32 devices in a mesh: face: 2 (over core), sub: 16 (over z, y, x).
Axes of the slice: x: 2, y: 2, z: 4, core: 2. Of those that a mesh axis runs over, the one named last changes fastest.
Arguments:
- features: bfloat16 [768, 24, 192], P(('face', 'sub')), may hold values from -6 to 6
- w_first: bfloat16 [3, 3, 192, 192], replicated, may hold values from -0.15625 to 0.15625
- b_first: float32 [192], replicated, may hold values from -3 to 3
- w_second: bfloat16 [3, 3, 192, 192], replicated, may hold values from -0.15625 to 0.15625
- neighbours: int32 [32, 4], replicated, may hold values from 0 to 31, as said below
- rotations: int32 [32, 4], replicated, may hold values from 0 to 3
- cotangent: bfloat16 [384, 12, 192], P(('face', 'sub')), may hold values from -6 to 6
Outputs:
- pooled: bfloat16 [384, 12, 192], P(('face', 'sub'))
- grad_input: bfloat16 [768, 24, 192], P(('face', 'sub'))
- grad_w1: float32 [3, 3, 192, 192], replicated
- grad_b1: float32 [192], replicated
- grad_w2: float32 [3, 3, 192, 192], replicated
The draws below stay inside these ranges and needn't reach their ends.
Inputs may be any that keep to these rules, and one draw needn't show every extreme that they name: neighbours[d, e] is a tile f * 16 + s other than d; it has the same f as d or the same s as d; two tiles of the same f share at most one edge, and no tile names the same tile of its own f at two edges.
All inputs are finite; a program needn't handle non-finite values.
Results may differ from the reference program's by a relative error of at most 0.012.
Values may be sent and summed in bfloat16 or wider, within the bound.
A program may use at most 64 MiB of HBM per device.

```python
import math
import jax
import jax.numpy as jnp
import numpy as np
from jax import lax

C = 192
TB = 24
HALF = 12
DEVS = 32
ROWS = 768
HALF_ROWS = 384
N_FACE = 2
N_SUB = 16


def draw_neighbours(key, part):
    bit_count = N_SUB.bit_length() - 1
    places = []
    for sub_pos in range(N_SUB):
        column = 0
        row_pos = 0
        for bit_pos in range(bit_count):
            if bit_pos % 2 == 0:
                column = column + ((sub_pos >> bit_pos & 1) << bit_pos // 2)
            else:
                row_pos = row_pos + ((sub_pos >> bit_pos & 1) << bit_pos // 2)
        places.append((row_pos, column))
    finder = {}
    for sub_pos in range(N_SUB):
        finder[places[sub_pos]] = sub_pos
    step_list = [(-1, 0), (0, 1), (1, 0), (0, -1)]
    inside_sub = np.zeros((N_SUB, 4), np.int32)
    inside_flag = np.zeros((N_SUB, 4), np.int32)
    for sub_pos in range(N_SUB):
        for border in range(4):
            target = (places[sub_pos][0] + step_list[border][0], places[sub_pos][1] + step_list[border][1])
            if target in finder:
                inside_sub[sub_pos, border] = finder[target]
                inside_flag[sub_pos, border] = 1
            else:
                inside_sub[sub_pos, border] = sub_pos
    positions = jnp.arange(N_SUB, dtype=jnp.int32)
    shuffled = jax.random.permutation(jax.random.fold_in(key, 13), N_SUB).astype(jnp.int32)
    wanted = (shuffled[0] + N_SUB // 2) % N_SUB
    where_wanted = jnp.sum(jnp.where(shuffled == wanted, positions, 0)).astype(jnp.int32)
    second_label = shuffled[1]
    labels = jnp.where(positions == 1, wanted, jnp.where(positions == where_wanted, second_label, shuffled)).astype(jnp.int32)
    inside_label = labels[jnp.asarray(inside_sub)]
    face_order = jax.random.permutation(jax.random.fold_in(key, 11), N_FACE).astype(jnp.int32)
    inverse = jnp.argsort(face_order).astype(jnp.int32)
    shifts = jax.random.randint(jax.random.fold_in(key, 12), (4,), 1, N_FACE).astype(jnp.int32)
    partner = inverse[(face_order[:, None] + shifts[None, :]) % N_FACE]
    face_ids = jnp.arange(N_FACE, dtype=jnp.int32)
    owner_face = jnp.where(jnp.asarray(inside_flag)[None] == 1, face_ids[:, None, None], partner[:, None, :])
    by_position = owner_face * N_SUB + inside_label[None]
    result = jnp.zeros((N_FACE, N_SUB, 4), jnp.int32).at[:, labels].set(by_position)
    return result.reshape(N_FACE * N_SUB, 4).astype(jnp.int32)


def with_ends(entries, own_key, least, largest):
    index_at = [jax.random.randint(jax.random.fold_in(own_key, axis), (), 0, length) for axis, length in enumerate(entries.shape)]
    widest = entries.shape.index(max(entries.shape))
    next_to = index_at[:widest] + [(index_at[widest] + 1) % entries.shape[widest]] + index_at[widest + 1:]
    return entries.at[tuple(index_at)].set(least).at[tuple(next_to)].set(largest)


def block_levels(key, shape, cuts, least, high):
    level = 1.0
    for position, blocks in cuts:
        steps = jax.random.uniform(jax.random.fold_in(jax.random.fold_in(key, 6), position), (blocks,), jnp.float32, least / len(cuts), high / len(cuts))
        level = level * jnp.repeat(jnp.exp(steps), shape[position] // blocks).reshape((-1,) + (1,) * (len(shape) - 1 - position))
    return level


def gaussian(rng, shape, deviation, limit, pieces=(), held_as=jnp.bfloat16):
    values = jax.random.normal(rng, shape, jnp.float32) * deviation
    if len(pieces) > 0:
        values = block_levels(rng, shape, pieces, -0.22, 0.18) * values
    return jnp.clip(values, min=-limit, max=limit).astype(held_as)


def setup_inputs(seed: int = 0) -> dict:
    arg_keys = jax.random.split(jax.random.key(seed), 8)
    return {
        "features": gaussian(arg_keys[0], (ROWS, TB, C), 1.0, 6.0, ((0, 32),)),
        "w_first": gaussian(arg_keys[1], (3, 3, C, C), (9 * C) ** -0.5, 0.15625),
        "b_first": gaussian(arg_keys[2], (C,), 0.5, 3.0, (), jnp.float32),
        "w_second": gaussian(arg_keys[3], (3, 3, C, C), (9 * C) ** -0.5, 0.15625),
        "neighbours": draw_neighbours(jax.random.fold_in(arg_keys[7], 71), 0),
        "rotations": with_ends(jax.random.randint(arg_keys[5], (DEVS, 4), 0, 4), jax.random.fold_in(arg_keys[5], 1), 0, 3).astype(jnp.int32),
        "cotangent": gaussian(arg_keys[6], (HALF_ROWS, HALF, C), 1.0, 6.0, ((0, 32),)),
    }


def rim_lookup():
    return np.array([[[0, 0], [1, 0], [2, 0], [3, 0]], [[1, 0], [2, 1], [3, 0], [0, 1]], [[2, 1], [3, 1], [0, 1], [1, 1]], [[3, 1], [0, 0], [1, 1], [2, 0]]], np.int32)

def rim_codes(rotations):
    lookup = rim_lookup()[:, [2, 3, 0, 1], :]
    anchor_tab = jnp.asarray(lookup[:, :, 0])
    flip_tab = jnp.asarray(lookup[:, :, 1])
    border_ids = jnp.arange(4, dtype=jnp.int32)
    anchors = anchor_tab[rotations, border_ids[None, :]]
    flip_codes = flip_tab[rotations, border_ids[None, :]]
    return (anchors, flip_codes)

def pad_tiles(tile_set, neighbours, rotations):
    anchors, flip_codes = rim_codes(rotations)
    edge_rows = jnp.stack([tile_set[:, 0], tile_set[:, :, -1], tile_set[:, -1], tile_set[:, :, 0]], axis=1)
    picked = edge_rows[neighbours, anchors]
    picked = jnp.where(flip_codes[:, :, None, None] == 1, picked[:, :, ::-1], picked)
    padded = jnp.pad(tile_set, ((0, 0), (1, 1), (1, 1), (0, 0)))
    padded = padded.at[:, 0, 1:-1].set(picked[:, 0])
    padded = padded.at[:, 1:-1, -1].set(picked[:, 1])
    padded = padded.at[:, -1, 1:-1].set(picked[:, 2])
    padded = padded.at[:, 1:-1, 0].set(picked[:, 3])
    return padded

def correlate(padded, weights):
    extent = padded.shape[1] - 2
    summed = jnp.zeros((padded.shape[0], extent, extent, weights.shape[3]), jnp.float32)
    for row_off in range(3):
        for col_off in range(3):
            window = padded[:, row_off:row_off + extent, col_off:col_off + extent]
            summed = summed + jnp.einsum('dijc,co->dijo', window, weights[row_off, col_off].astype(jnp.float32))
    return summed

def spread_back(grads, weights):
    extent = grads.shape[1]
    summed = jnp.zeros((grads.shape[0], extent + 2, extent + 2, weights.shape[2]), jnp.float32)
    for row_off in range(3):
        for col_off in range(3):
            portion = jnp.einsum('dijo,co->dijc', grads, weights[row_off, col_off].astype(jnp.float32))
            summed = summed.at[:, row_off:row_off + extent, col_off:col_off + extent].add(portion)
    return summed

def weight_grad(padded, grads):
    extent = grads.shape[1]
    blocks_out = []
    for row_off in range(3):
        for col_off in range(3):
            window = padded[:, row_off:row_off + extent, col_off:col_off + extent]
            blocks_out.append(jnp.einsum('dijc,dijo->co', window, grads))
    return jnp.stack(blocks_out, axis=0).reshape(3, 3, padded.shape[3], grads.shape[3])

def fold_back(summed, neighbours, rotations):
    anchors, flip_codes = rim_codes(rotations)
    middle = summed[:, 1:-1, 1:-1]
    outer = jnp.stack([summed[:, 0, 1:-1], summed[:, 1:-1, -1], summed[:, -1, 1:-1], summed[:, 1:-1, 0]], axis=1)
    outer = jnp.where(flip_codes[:, :, None, None] == 1, outer[:, :, ::-1], outer)
    arrived = jnp.zeros_like(outer).at[neighbours, anchors].add(outer)
    middle = middle.at[:, 0].add(arrived[:, 0])
    middle = middle.at[:, :, -1].add(arrived[:, 1])
    middle = middle.at[:, -1].add(arrived[:, 2])
    middle = middle.at[:, :, 0].add(arrived[:, 3])
    return middle

def reference(features, w_first, b_first, w_second, neighbours, rotations, cotangent):
    tile_set = features.reshape(DEVS, TB, TB, C).astype(jnp.float32)
    padded_in = pad_tiles(tile_set, neighbours, rotations)
    hidden = correlate(padded_in, w_first) + b_first
    active = lax.optimization_barrier(jax.nn.silu(hidden).astype(jnp.bfloat16)).astype(jnp.float32)
    padded_act = pad_tiles(active, neighbours, rotations)
    second = correlate(padded_act, w_second)
    summed_out = tile_set + second
    pooled = summed_out.reshape(DEVS, HALF, 2, HALF, 2, C).mean(axis=(2, 4)).astype(jnp.bfloat16)
    upward = cotangent.reshape(DEVS, HALF, HALF, C).astype(jnp.float32) * 0.25
    grad_out = jnp.broadcast_to(upward[:, :, None, :, None, :], (DEVS, HALF, 2, HALF, 2, C)).reshape(DEVS, TB, TB, C)
    sum_w2 = weight_grad(padded_act, grad_out)
    grad_active = fold_back(spread_back(grad_out, w_second), neighbours, rotations)
    grad_active = lax.optimization_barrier(grad_active.astype(jnp.bfloat16)).astype(jnp.float32)
    sigmoid_h = jax.nn.sigmoid(hidden)
    grad_hidden = grad_active * sigmoid_h * (1.0 + hidden * (1.0 - sigmoid_h))
    grad_hidden = lax.optimization_barrier(grad_hidden.astype(jnp.bfloat16)).astype(jnp.float32)
    sum_b1 = lax.optimization_barrier(jnp.sum(grad_hidden, axis=(0, 1, 2)))
    sum_w1 = weight_grad(padded_in, grad_hidden)
    grad_input = fold_back(spread_back(grad_hidden, w_first), neighbours, rotations) + grad_out
    grad_scale = 1.0 / math.sqrt(DEVS * TB * TB)
    return (pooled.reshape(DEVS * HALF, HALF, C), grad_input.astype(jnp.bfloat16).reshape(DEVS * TB, TB, C), sum_w1 * grad_scale, sum_b1 * grad_scale, sum_w2 * grad_scale)
```

```python
import functools
import math

import jax
import jax.numpy as jnp
from jax import lax
from jax.experimental import pallas as pl
from jax.experimental.pallas import tpu as pltpu
from jax.sharding import PartitionSpec as P

LANES = 128
W = 32
F32, BF16 = jnp.float32, jnp.bfloat16
MESH = pl.DeviceIdType.MESH


def iota(shape, dim):
    return lax.broadcasted_iota(jnp.int32, shape, dim)


def hot(mask):
    return jnp.where(mask, 1.0, 0.0).astype(BF16)


def dot(a, b, ca=1, cb=0):
    return lax.dot_general(a, b, (((ca,), (cb,)), ((), ())), preferred_element_type=F32)


def split(x):
    hi = x.astype(BF16)
    return hi, (x - hi.astype(F32)).astype(BF16)


def rim_pos(q, extent, pad):
    e, p = q >> 5, (q & (W - 1)) + pad
    far = extent - 1 + 2 * pad
    pos = jnp.where(e == 0, p, jnp.where(e == 1, p * W + far, jnp.where(e == 2, far * W + p, p * W)))
    return jnp.where((q & (W - 1)) < extent, pos, -1)


def pool_pos(r):
    return ((r >> 6) << 4) + ((r & (W - 1)) >> 1)


def kernel(S, F, chunk, scale, nbr, rot, feat, cot, w1, b1, w2,
           pooled, gin, gath,
           send_mat, recv_mat, pad_in, pad_act, gpad1, gpad2, cotp,
           win_in, win_act, gs1, gs2, hidden, second, pg, gact,
           ex_out, ex_in, wf, wb, w1in, red, accf, w2in, red2, acc2, w3in,
           ex_ss, ex_rs, w_ss, w_rs):
    T, C = feat.shape[0], feat.shape[2]
    H = T // 2
    face, sub = lax.axis_index("face"), lax.axis_index("sub")
    me = face * S + sub
    part = chunk * S
    A = 4 if S % 4 == 0 else 1
    B = S // A
    a_id, b_id = sub // B, lax.rem(sub, B)
    group = chunk * A
    M, MP = T * W, (T + 2) * W

    def peers(count, mine, body):
        def step(d, c):
            body(lax.rem(mine + d, count))
            return c
        lax.fori_loop(1, count, step, 0)

    barrier = pltpu.get_barrier_semaphore()
    peers(S, sub, lambda j: pl.semaphore_signal(barrier, inc=1, device_id=(face, j), device_id_type=MESH))
    peers(F, face, lambda f: pl.semaphore_signal(barrier, inc=1, device_id=(f, sub), device_id_type=MESH))

    p32 = iota((W, 4 * W), 0)
    c32 = iota((W, 4 * W), 1)

    def put_slot(k, hit, src, flip, edge):
        tgt = jnp.where(flip == 1, src * W + T - 1 - p32, src * W + p32)
        base = pl.multiple_of(k * W, W)
        send_mat[pl.ds(base, W), :] = hot((c32 == tgt) & (p32 < T) & (hit == 1))
        recv_mat[pl.ds(base, W), :] = hot((c32 == edge * W + p32) & (p32 < T) & (edge >= 0))

    def edge_code(tile, e):
        r = rot[e, tile]
        x = (e + 2) % 4
        src = (x + r) & 3
        odd = x % 2
        flip = jnp.where(r == 2, 1, jnp.where(r == 1, odd, jnp.where(r == 3, 1 - odd, 0)))
        return nbr[e, tile] == me, src, flip

    def in_face(j, c):
        hit, src, flip, edge = jnp.int32(0), jnp.int32(0), jnp.int32(0), jnp.int32(-1)
        for e in range(4):
            h, s, f = edge_code(face * S + j, e)
            hit = jnp.where(h, 1, hit)
            src = jnp.where(h, s, src)
            flip = jnp.where(h, f, flip)
            edge = jnp.where(nbr[e, me] == face * S + j, e, edge)
        put_slot(j, hit, src, flip, edge)
        return c

    lax.fori_loop(0, S, in_face, 0)

    def cross(f, c):
        for e in range(4):
            h, s, fl = edge_code(f * S + sub, e)
            other = f != face
            hit = jnp.where(h & other, 1, 0)
            edge = jnp.where((nbr[e, me] == f * S + sub) & other, e, -1)
            put_slot(S + f * 4 + e, hit, s, fl, edge)
        return c

    lax.fori_loop(0, F, cross, 0)

    for ph in range(4):
        ex_in[ph, pl.ds(pl.multiple_of(sub * W, W), W), :] = jnp.zeros((W, C), BF16)
        ex_in[ph, pl.ds(pl.multiple_of((S + 4 * face) * W, W), 4 * W), :] = jnp.zeros((4 * W, C), BF16)

    def ex_sub(ph, j, s_in):
        return pltpu.make_async_remote_copy(
            src_ref=ex_out.at[ph, pl.ds(pl.multiple_of(j * W, W), W), :],
            dst_ref=ex_in.at[ph, pl.ds(pl.multiple_of(s_in * W, W), W), :],
            send_sem=ex_ss.at[ph], recv_sem=ex_rs.at[ph],
            device_id=(face, j), device_id_type=MESH)

    def ex_face(ph, f, f_in):
        return pltpu.make_async_remote_copy(
            src_ref=ex_out.at[ph, pl.ds(pl.multiple_of((S + 4 * f) * W, W), 4 * W), :],
            dst_ref=ex_in.at[ph, pl.ds(pl.multiple_of((S + 4 * f_in) * W, W), 4 * W), :],
            send_sem=ex_ss.at[ph], recv_sem=ex_rs.at[ph],
            device_id=(f, sub), device_id_type=MESH)

    def ex_start(ph, mat, rims):
        ex_out[ph] = dot(mat[...], rims).astype(BF16)
        peers(S, sub, lambda j: ex_sub(ph, j, sub).start())
        peers(F, face, lambda f: ex_face(ph, f, face).start())

    def take(ref, sem):
        pltpu.make_async_copy(ref, ref, sem).wait()

    ex_rows = (S - 1) * W + (F - 1) * 4 * W

    def ex_wait(ph, mat):
        take(ex_in.at[ph, 0:ex_rows, :], ex_rs.at[ph])
        return dot(mat[...], ex_in[ph], 0, 0)

    def ex_drain(ph):
        take(ex_out.at[ph, 0:ex_rows, :], ex_ss.at[ph])

    own_rims = hot(iota((4 * W, M), 1) == rim_pos(iota((4 * W, 1), 0), T, 0))
    pad_rims = hot(iota((4 * W, MP), 1) == rim_pos(iota((4 * W, 1), 0), T, 1))
    own_place = hot(iota((M, 4 * W), 0) == rim_pos(iota((1, 4 * W), 1), T, 0))
    pad_place = hot(iota((MP, 4 * W), 0) == rim_pos(iota((1, 4 * W), 1), T, 1))

    def windows(src, dst, rows):
        for b in range(3):
            dst[b] = src[:, b:b + W, :].reshape(rows * W, C).astype(BF16)

    def add_halo(padded, halo):
        placed = dot(pad_place, halo.astype(BF16)).reshape(T + 2, W, C)
        padded[:, 0:W, :] = padded[:, 0:W, :] + placed

    def conv(win, wt, out, rows, back):
        half = rows

        def step(i, c):
            acc = None
            for a in range(3):
                for b in range(3):
                    off = pl.multiple_of(i * half, 16) + a * W
                    x = win[b, pl.ds(pl.multiple_of(off, 16), half), :]
                    tap = (2 - a) * 3 + 2 - b if back else a * 3 + b
                    d = dot(x, wt[tap * C:(tap + 1) * C, :], 1, 1 if back else 0)
                    acc = d if acc is None else acc + d
            out[pl.ds(pl.multiple_of(i * half, 16), half), :] = acc
            return c

        lax.fori_loop(0, 1, step, 0)

    def put(k, r, v):
        wf[k, r:r + v.shape[0], :] = v
        wb[k, r:r + v.shape[0], :] = v.astype(BF16)

    def weight_grad(k, win, gs):
        odd = None
        for t in range(9):
            a, b = t // 3, t % 3
            v = dot(win[b], gs[2, (2 - a) * W:(2 - a) * W + MP, :], 0, 0)
            put(k, t * C, v[:, 0:LANES])
            rest = v[:, LANES:C]
            if t % 2 == 0:
                odd = rest
            if t % 2 == 1 or t == 8:
                pair = jnp.concatenate([odd, rest], axis=1)
                put(k, (9 + t // 2) * C, pair)

    pad_in[...] = jnp.zeros(pad_in.shape, F32)
    pad_in[1:T + 1, 1:T + 1, :] = feat[...].astype(F32)
    flat_in = pad_in[1:T + 1, 1:W + 1, :].reshape(M, C)
    rims = dot(own_rims, flat_in.astype(BF16)).astype(BF16)
    pl.semaphore_wait(barrier, S + F - 2)
    ex_start(0, send_mat, rims)

    cotp[...] = jnp.zeros(cotp.shape, F32)
    cotp[:, 0:H, :] = cot[...].astype(F32)
    spread = hot(pool_pos(iota((M, 1), 0)) == iota((M, H * 16), 1))
    up = dot(spread, cotp[...].reshape(H * 16, C).astype(BF16)) * 0.25
    gpad2[...] = jnp.zeros(gpad2.shape, F32)
    gpad2[2:T + 2, 2:T + 2, :] = up.reshape(T, W, C)[:, 0:T, :]
    windows(gpad2, gs2, T + 4)
    conv(gs2, w2, pg, MP, True)
    rims = dot(pad_rims, pg[...].astype(BF16)).astype(BF16)
    ex_start(2, recv_mat, rims)
    gact[...] = pg[...].reshape(T + 2, W, C)[1:T + 1]
    pad_act[...] = jnp.zeros(pad_act.shape, F32)
    gpad1[...] = jnp.zeros(gpad1.shape, F32)

    add_halo(pad_in, ex_wait(0, recv_mat))
    windows(pad_in, win_in, T + 2)
    conv(win_in, w1, hidden, M, False)
    hid = hidden[...] + b1[...]
    sig = 1.0 / (1.0 + jnp.exp(-hid))
    act = (hid * sig).astype(BF16)
    rims = dot(own_rims, act).astype(BF16)
    ex_start(1, send_mat, rims)
    pad_act[1:T + 1, 1:T + 1, :] = act.astype(F32).reshape(T, W, C)[:, 0:T, :]

    def fold(middle, arrived):
        hi, lo = split(arrived)
        back = dot(own_place, hi) + dot(own_place, lo)
        return middle[:, 1:T + 1, :] + back.reshape(T, W, C)[:, 0:T, :]

    ga = fold(gact, ex_wait(2, send_mat)).astype(BF16).astype(F32)
    slope = (sig * (1.0 + hid * (1.0 - sig))).reshape(T, W, C)[:, 0:T, :]
    gh = (ga * slope).astype(BF16).astype(F32)
    gpad1[2:T + 2, 2:T + 2, :] = gh
    windows(gpad1, gs1, T + 4)

    rows = wf.shape[1]

    def face_copy(k, f, f_in):
        return pltpu.make_async_remote_copy(
            src_ref=wb.at[k, pl.ds(pl.multiple_of(f * part, 16), part), :],
            dst_ref=w1in.at[k, f_in],
            send_sem=w_ss.at[k, 0], recv_sem=w_rs.at[k, 0],
            device_id=(f, sub), device_id_type=MESH)

    def b_copy(k, j, j_in):
        return pltpu.make_async_remote_copy(
            src_ref=red.at[k, pl.ds(pl.multiple_of(j * group, 16), group), :],
            dst_ref=w2in.at[k, j_in],
            send_sem=w_ss.at[k, 1], recv_sem=w_rs.at[k, 1],
            device_id=(face, a_id * B + j), device_id_type=MESH)

    def a_copy(k, j, j_in):
        return pltpu.make_async_remote_copy(
            src_ref=red2.at[k, pl.ds(pl.multiple_of(j * chunk, 16), chunk), :],
            dst_ref=w3in.at[k, j_in],
            send_sem=w_ss.at[k, 2], recv_sem=w_rs.at[k, 2],
            device_id=(face, j * B + b_id), device_id_type=MESH)

    def spot(k, start, size):
        return gath.at[k, pl.ds(pl.multiple_of(start, 16), size), :]

    def a_gather(k, j, own):
        place = spot(k, face * part + b_id * group + own * chunk, chunk)
        return pltpu.make_async_remote_copy(
            src_ref=place, dst_ref=place,
            send_sem=w_ss.at[k, 3], recv_sem=w_rs.at[k, 3],
            device_id=(face, j * B + b_id), device_id_type=MESH)

    def b_gather(k, j, own):
        place = spot(k, face * part + own * group, group)
        return pltpu.make_async_remote_copy(
            src_ref=place, dst_ref=place,
            send_sem=w_ss.at[k, 4], recv_sem=w_rs.at[k, 4],
            device_id=(face, a_id * B + j), device_id_type=MESH)

    def face_gather(k, f, own):
        place = spot(k, own * part, part)
        return pltpu.make_async_remote_copy(
            src_ref=place, dst_ref=place,
            send_sem=w_ss.at[k, 5], recv_sem=w_rs.at[k, 5],
            device_id=(f, sub), device_id_type=MESH)

    sizes = ((F - 1) * part, (B - 1) * group, (A - 1) * chunk, (A - 1) * chunk, (B - 1) * group, (F - 1) * part)

    counts = (F - 1, B - 1, A - 1)

    def arrived_all(k, st):
        if sizes[st]:
            slots = (w1in, w2in, w3in)
            take(slots[st].at[k, 0:counts[st]] if st < 3 else gath.at[k, 0:sizes[st], :], w_rs.at[k, st])

    def reduce_start(k):
        peers(F, face, lambda f: face_copy(k, f, face).start())

    def summed(first, count, mine, ref, k):
        def step(d, tot):
            return tot + ref[k, lax.rem(mine + d, count)].astype(F32)
        return lax.fori_loop(1, count, step, first)

    def reduce_b(k):
        arrived_all(k, 0)
        for r in range(B):
            at = pl.ds(pl.multiple_of(face * part + r * group, 16), group)
            tot = wf[k, at, :]
            for f in range(1, F):
                tot = tot + w1in[k, lax.rem(face + f, F), r * group:(r + 1) * group, :].astype(F32)
            accf[k, r * group:(r + 1) * group, :] = tot
            red[k, r * group:(r + 1) * group, :] = tot.astype(BF16)
        peers(B, b_id, lambda j: b_copy(k, j, b_id).start())

    def reduce_a(k):
        arrived_all(k, 1)
        tot = summed(accf[k, pl.ds(pl.multiple_of(b_id * group, 16), group), :], B, b_id, w2in, k)
        acc2[k] = tot
        red2[k] = tot.astype(BF16)
        peers(A, a_id, lambda j: a_copy(k, j, a_id).start())

    def gather_a(k):
        arrived_all(k, 2)
        tot = summed(acc2[k, pl.ds(pl.multiple_of(a_id * chunk, 16), chunk), :], A, a_id, w3in, k)
        own = pl.ds(pl.multiple_of(face * part + b_id * group + a_id * chunk, 16), chunk)
        gath[k, own, :] = (tot * scale).astype(BF16)
        peers(A, a_id, lambda j: a_gather(k, j, a_id).start())

    def gather_b(k):
        arrived_all(k, 3)
        peers(B, b_id, lambda j: b_gather(k, j, b_id).start())

    def gather_face(k):
        arrived_all(k, 4)
        peers(F, face, lambda f: face_gather(k, f, face).start())

    def gather_end(k):
        arrived_all(k, 5)

    def drain(k):
        for st in range(6):
            if sizes[st]:
                take((wb, red, red2, gath, gath, gath)[st].at[k, 0:sizes[st], :], w_ss.at[k, st])

    for k in range(2):
        put(k, 14 * C, jnp.zeros((rows - 14 * C, LANES), F32))
    weight_grad(0, win_in, gs1)
    bias = jnp.sum(jnp.sum(gh, axis=0), axis=0, keepdims=True)
    bias = jnp.concatenate([bias, jnp.zeros((1, 2 * LANES - C), F32)], axis=1)
    line = iota((16, LANES), 0)
    put(0, 14 * C, jnp.where(line == 0, bias[:, 0:LANES], jnp.where(line == 1, bias[:, LANES:], 0.0)))
    reduce_start(0)

    add_halo(pad_act, ex_wait(1, recv_mat))
    windows(pad_act, win_act, T + 2)
    reduce_b(0)
    weight_grad(1, win_act, gs2)
    reduce_start(1)
    conv(gs1, w1, pg, MP, True)
    rims = dot(pad_rims, pg[...].astype(BF16)).astype(BF16)
    ex_start(3, recv_mat, rims)
    reduce_a(0)
    reduce_b(1)
    conv(win_act, w2, second, M, False)
    gather_a(0)
    hi, lo = split(second[...] + pad_in[1:T + 1, 1:W + 1, :].reshape(M, C))
    mean = hot(pool_pos(iota((1, M), 1)) == iota((H * 16, M), 0))
    down = (dot(mean, hi) + dot(mean, lo)) * 0.25
    pooled[...] = down.reshape(H, 16, C)[:, 0:H, :].astype(BF16)
    reduce_a(1)
    gather_b(0)
    gact[...] = pg[...].reshape(T + 2, W, C)[1:T + 1]
    total = fold(gact, ex_wait(3, send_mat)) + gpad2[2:T + 2, 2:T + 2, :]
    gin[...] = total.astype(BF16)
    gather_a(1)
    gather_face(0)
    gather_b(1)
    gather_end(0)
    gather_face(1)
    gather_end(1)
    for ph in range(4):
        ex_drain(ph)
    for k in range(2):
        drain(k)


def finish(C, pooled_in, gin_in, gath, pooled, gin, gw1, gb1, gw2):
    pooled[...] = pooled_in[...]
    gin[...] = gin_in[...]
    for k, out in ((0, gw1), (1, gw2)):
        for t in range(9):
            left = gath[k, t * C:(t + 1) * C, :].astype(F32)
            pair = gath[k, (9 + t // 2) * C:(10 + t // 2) * C, :].astype(F32)
            half = C - LANES
            right = pair[:, 0:half] if t % 2 == 0 else pair[:, half:2 * half]
            out[t // 3, t % 3, :, 0:LANES] = left
            out[t // 3, t % 3, :, LANES:C] = right
    bias = gath[0, 14 * C:14 * C + 16, :].astype(F32)
    gb1[:, 0:LANES] = bias[0:1]
    gb1[:, LANES:C] = bias[1:2, 0:C - LANES]


def local(S, F, features, w_first, b_first, w_second, neighbours, rotations, cotangent):
    T, C = features.shape[1], features.shape[2]
    H = T // 2
    D = neighbours.shape[0]
    chunk = -(-(14 * C + 16) // (16 * D)) * 16
    A = 4 if S % 4 == 0 else 1
    B = S // A
    rows, part = chunk * D, chunk * S
    K = (S + 4 * F) * W
    scale = 1.0 / math.sqrt(D * T * T)
    vm = pl.BlockSpec(memory_space=pltpu.VMEM)
    sm = pl.BlockSpec(memory_space=pltpu.SMEM)
    pooled, gin, gath = pl.pallas_call(
        functools.partial(kernel, S, F, chunk, scale),
        out_shape=(
            pltpu.VMEM((H, H, C), BF16),
            pltpu.VMEM((T, T, C), BF16),
            pltpu.VMEM((2, rows, LANES), BF16),
        ),
        in_specs=[sm, sm, vm, vm, vm, vm, vm],
        out_specs=(vm,) * 3,
        scratch_shapes=[
            pltpu.VMEM((K, 4 * W), BF16),
            pltpu.VMEM((K, 4 * W), BF16),
            pltpu.VMEM((T + 2, W + 8, C), F32),
            pltpu.VMEM((T + 2, W + 8, C), F32),
            pltpu.VMEM((T + 4, W + 8, C), F32),
            pltpu.VMEM((T + 4, W + 8, C), F32),
            pltpu.VMEM((H, 16, C), F32),
            pltpu.VMEM((3, (T + 2) * W, C), BF16),
            pltpu.VMEM((3, (T + 2) * W, C), BF16),
            pltpu.VMEM((3, (T + 4) * W, C), BF16),
            pltpu.VMEM((3, (T + 4) * W, C), BF16),
            pltpu.VMEM((T * W, C), F32),
            pltpu.VMEM((T * W, C), F32),
            pltpu.VMEM(((T + 2) * W, C), F32),
            pltpu.VMEM((T, W, C), F32),
            pltpu.VMEM((4, K, C), BF16),
            pltpu.VMEM((4, K, C), BF16),
            pltpu.VMEM((2, rows, LANES), F32),
            pltpu.VMEM((2, rows, LANES), BF16),
            pltpu.VMEM((2, F, part, LANES), BF16),
            pltpu.VMEM((2, part, LANES), BF16),
            pltpu.VMEM((2, part, LANES), F32),
            pltpu.VMEM((2, B, A * chunk, LANES), BF16),
            pltpu.VMEM((2, A * chunk, LANES), BF16),
            pltpu.VMEM((2, A * chunk, LANES), F32),
            pltpu.VMEM((2, A, chunk, LANES), BF16),
            pltpu.SemaphoreType.DMA((4,)),
            pltpu.SemaphoreType.DMA((4,)),
            pltpu.SemaphoreType.DMA((2, 6)),
            pltpu.SemaphoreType.DMA((2, 6)),
        ],
        compiler_params=pltpu.CompilerParams(
            collective_id=0, has_side_effects=True, vmem_limit_bytes=56 * 1024 * 1024
        ),
        name="level",
    )(
        neighbours.T, rotations.T, features, cotangent,
        w_first.reshape(9 * C, C), b_first.reshape(1, C), w_second.reshape(9 * C, C),
    )
    pooled, gin, gw1, gb1, gw2 = pl.pallas_call(
        functools.partial(finish, C),
        out_shape=(
            jax.ShapeDtypeStruct((H, H, C), BF16),
            jax.ShapeDtypeStruct((T, T, C), BF16),
            jax.ShapeDtypeStruct((3, 3, C, C), F32),
            jax.ShapeDtypeStruct((1, C), F32),
            jax.ShapeDtypeStruct((3, 3, C, C), F32),
        ),
        in_specs=[vm] * 3,
        out_specs=(vm,) * 5,
        compiler_params=pltpu.CompilerParams(vmem_limit_bytes=24 * 1024 * 1024),
        name="finish",
    )(pooled, gin, gath)
    return (pooled, gin, gw1, gb1.reshape(C), gw2)


def solution(mesh):
    tiles = P(("face", "sub"), None, None)
    return jax.shard_map(
        functools.partial(local, mesh.shape["sub"], mesh.shape["face"]),
        mesh=mesh,
        in_specs=(tiles, P(), P(), P(), P(), P(), tiles),
        out_specs=(tiles, tiles, P(), P(), P()),
        check_vma=False,
    )
```

```python
import functools
import math

import jax
import jax.numpy as jnp
from jax import lax
from jax.experimental import pallas as pl
from jax.experimental.pallas import tpu as pltpu
from jax.sharding import PartitionSpec as P

LANES = 128
W = 32
LOW = 16
F32, BF16 = jnp.float32, jnp.bfloat16
MESH = pl.DeviceIdType.MESH


def iota(shape, dim):
    return lax.broadcasted_iota(jnp.int32, shape, dim)


def hot(mask):
    return jnp.where(mask, 1.0, 0.0).astype(BF16)


def dot(a, b, ca=1, cb=0):
    return lax.dot_general(a, b, (((ca,), (cb,)), ((), ())), preferred_element_type=F32)


def split(x):
    hi = x.astype(BF16)
    return hi, (x - hi.astype(F32)).astype(BF16)


def rim_pos(q, extent, pad):
    e, p = q >> 5, (q & (W - 1)) + pad
    far = extent - 1 + 2 * pad
    pos = jnp.where(e == 0, p, jnp.where(e == 1, p * W + far, jnp.where(e == 2, far * W + p, p * W)))
    return jnp.where((q & (W - 1)) < extent, pos, -1)


def pool_pos(r):
    return ((r >> 6) << 4) + ((r & (W - 1)) >> 1)


def kernel(S, F, chunk, scale, nbr_hbm, rot_hbm, feat_hbm, cot_hbm, w1_hbm, b1_hbm, w2_hbm,
           pooled, gin, gath,
           nbr, rot, feat, cot, w1, b1, w2,
           send_mat, recv_mat, send_low, recv_low, pad_in, pad_act, gpad1, gpad2, cotp,
           win_in, win_act, gs1, gs2, hidden, second, pg, gact,
           ex_out, ex_in, wf, wb, w1in, red, accf, w2in, red2, acc2, w3in,
           ex_ss, ex_rs, w_ss, w_rs, in_sem):
    T, C = feat.shape[0], feat.shape[2]
    H = T // 2
    face, sub = lax.axis_index("face"), lax.axis_index("sub")
    me = face * S + sub
    part = chunk * S
    A = 4 if S % 4 == 0 else 1
    B = S // A
    a_id, b_id = sub // B, lax.rem(sub, B)
    group = chunk * A
    M, MP = T * W, (T + 2) * W

    def peers(count, mine, body):
        def step(d, c):
            body(lax.rem(mine + d, count))
            return c
        lax.fori_loop(1, count, step, 0)

    barrier = pltpu.get_barrier_semaphore()
    peers(S, sub, lambda j: pl.semaphore_signal(barrier, inc=1, device_id=(face, j), device_id_type=MESH))
    peers(F, face, lambda f: pl.semaphore_signal(barrier, inc=1, device_id=(f, sub), device_id_type=MESH))

    def load(i):
        pairs = ((nbr_hbm, nbr), (rot_hbm, rot), (feat_hbm, feat), (w2_hbm, w2), (cot_hbm, cot), (w1_hbm, w1), (b1_hbm, b1))
        return pltpu.make_async_copy(pairs[i][0], pairs[i][1], in_sem.at[i])

    for i in (2, 0, 1, 3, 4, 5, 6):
        load(i).start()

    p32 = iota((W, 4 * W), 0)
    c32 = iota((W, 4 * W), 1)

    q16 = iota((LOW, 8 * W), 0)
    d16 = iota((LOW, 8 * W), 1)
    low_pix = q16 + jnp.where(d16 >= 4 * W, H, 0)
    low_col = d16 & (4 * W - 1)

    def put_send(k, hit, src, flip):
        tgt = jnp.where(flip == 1, src * W + T - 1 - p32, src * W + p32)
        send_mat[pl.ds(pl.multiple_of(k * W, W), W), :] = hot((c32 == tgt) & (p32 < T) & (hit == 1))
        tgt = jnp.where(flip == 1, src * W + T - 1 - low_pix, src * W + low_pix)
        send_low[pl.ds(pl.multiple_of(k * LOW, LOW), LOW), :] = hot((low_col == tgt) & (q16 < H) & (hit == 1))

    def put_recv(k, edge):
        recv_mat[pl.ds(pl.multiple_of(k * W, W), W), :] = hot((c32 == edge * W + p32) & (p32 < T) & (edge >= 0))
        recv_low[pl.ds(pl.multiple_of(k * LOW, LOW), LOW), :] = hot(
            (low_col == edge * W + low_pix) & (q16 < H) & (edge >= 0))

    def edge_code(tile, e):
        r = rot[e, tile]
        x = (e + 2) % 4
        src = (x + r) & 3
        odd = x % 2
        flip = jnp.where(r == 2, 1, jnp.where(r == 1, odd, jnp.where(r == 3, 1 - odd, 0)))
        return nbr[e, tile] == me, src, flip

    def send_in_face(j, c):
        hit, src, flip = jnp.int32(0), jnp.int32(0), jnp.int32(0)
        for e in range(4):
            h, s, f = edge_code(face * S + j, e)
            hit = jnp.where(h, 1, hit)
            src = jnp.where(h, s, src)
            flip = jnp.where(h, f, flip)
        put_send(j, hit, src, flip)
        return c

    def send_cross(f, c):
        for e in range(4):
            h, s, fl = edge_code(f * S + sub, e)
            put_send(S + f * 4 + e, jnp.where(h & (f != face), 1, 0), s, fl)
        return c

    def recv_in_face(j, c):
        edge = jnp.int32(-1)
        for e in range(4):
            edge = jnp.where(nbr[e, me] == face * S + j, e, edge)
        put_recv(j, edge)
        return c

    def recv_cross(f, c):
        for e in range(4):
            put_recv(S + f * 4 + e, jnp.where((nbr[e, me] == f * S + sub) & (f != face), e, -1))
        return c

    def ex_sub(ph, j, s_in):
        return pltpu.make_async_remote_copy(
            src_ref=ex_out.at[ph, j], dst_ref=ex_in.at[ph, s_in],
            send_sem=ex_ss.at[ph], recv_sem=ex_rs.at[ph],
            device_id=(face, j), device_id_type=MESH)

    def ex_face(ph, f, f_in):
        return pltpu.make_async_remote_copy(
            src_ref=ex_out.at[ph, pl.ds(S + 4 * f, 4)], dst_ref=ex_in.at[ph, pl.ds(S + 4 * f_in, 4)],
            send_sem=ex_ss.at[ph], recv_sem=ex_rs.at[ph],
            device_id=(f, sub), device_id_type=MESH)

    slots = S + 4 * F
    R = C - LANES

    def ex_start(ph, mat, low, rims):
        zero = jnp.zeros((4 * W, R), BF16)
        wide = jnp.concatenate([
            jnp.concatenate([rims[:, LANES:C], zero], axis=1),
            jnp.concatenate([zero, rims[:, LANES:C]], axis=1)], axis=0)
        ex_out[ph, :, 0:W, :] = dot(mat[...], rims[:, 0:LANES]).astype(BF16).reshape(slots, W, LANES)
        ex_out[ph, :, W:W + LOW, :] = dot(low[...], wide).astype(BF16).reshape(slots, LOW, LANES)
        peers(F, face, lambda f: ex_face(ph, f, face).start())
        peers(S, sub, lambda j: ex_sub(ph, j, sub).start())

    def take(ref, sem):
        pltpu.make_async_copy(ref, ref, sem).wait()

    ex_count = S - 1 + (F - 1) * 4

    def ex_wait(ph, mat, low):
        take(ex_in.at[ph, 0:ex_count], ex_rs.at[ph])
        left = dot(mat[...], ex_in[ph, :, 0:W, :].reshape(slots * W, LANES), 0, 0)
        rest = dot(low[...], ex_in[ph, :, W:W + LOW, :].reshape(slots * LOW, LANES), 0, 0)
        rest = rest[0:4 * W, 0:R] + rest[4 * W:8 * W, R:2 * R]
        return jnp.concatenate([left, rest], axis=1)

    def ex_drain(ph):
        take(ex_out.at[ph, 0:ex_count], ex_ss.at[ph])

    own_rims = hot(iota((4 * W, M), 1) == rim_pos(iota((4 * W, 1), 0), T, 0))

    def windows(src, dst, rows):
        for b in range(3):
            dst[b] = src[:, b:b + W, :].reshape(rows * W, C).astype(BF16)

    def add_halo(padded, halo):
        pad_place = hot(iota((MP, 4 * W), 0) == rim_pos(iota((1, 4 * W), 1), T, 1))
        placed = dot(pad_place, halo.astype(BF16)).reshape(T + 2, W, C)
        padded[:, 0:W, :] = padded[:, 0:W, :] + placed

    def conv(win, wt, out, lo, n, back):
        acc = None
        for a in range(3):
            for b in range(3):
                x = win[b, lo + a * W:lo + a * W + n, :]
                tap = (2 - a) * 3 + 2 - b if back else a * 3 + b
                d = dot(x, wt[tap * C:(tap + 1) * C, :], 1, 1 if back else 0)
                acc = d if acc is None else acc + d
        out[lo:lo + n, :] = acc

    def put(k, r, v):
        wf[k, r:r + v.shape[0], :] = v
        wb[k, r:r + v.shape[0], :] = v.astype(BF16)

    def weight_grad(k, win, gs):
        odd = None
        for t in range(9):
            a, b = t // 3, t % 3
            v = dot(win[b], gs[2, (2 - a) * W:(2 - a) * W + MP, :], 0, 0)
            put(k, t * C, v[:, 0:LANES])
            rest = v[:, LANES:C]
            if t % 2 == 0:
                odd = rest
            if t % 2 == 1 or t == 8:
                pair = jnp.concatenate([odd, rest], axis=1)
                put(k, (9 + t // 2) * C, pair)

    pad_in[...] = jnp.zeros(pad_in.shape, F32)
    load(2).wait()
    pad_in[1:T + 1, 1:T + 1, :] = feat[...].astype(F32)
    flat_in = pad_in[1:T + 1, 1:W + 1, :].reshape(M, C)
    rims = dot(own_rims, flat_in.astype(BF16)).astype(BF16)
    load(0).wait()
    load(1).wait()
    lax.fori_loop(0, S, send_in_face, 0)
    lax.fori_loop(0, F, send_cross, 0)
    pl.semaphore_wait(barrier, S + F - 2)
    ex_start(0, send_mat, send_low, rims)

    lax.fori_loop(0, S, recv_in_face, 0)
    lax.fori_loop(0, F, recv_cross, 0)
    cotp[...] = jnp.zeros(cotp.shape, F32)
    load(4).wait()
    cotp[:, 0:H, :] = cot[...].astype(F32)
    spread = hot(pool_pos(iota((M, 1), 0)) == iota((M, H * 16), 1))
    up = dot(spread, cotp[...].reshape(H * 16, C).astype(BF16)) * 0.25
    gpad2[...] = jnp.zeros(gpad2.shape, F32)
    gpad2[2:T + 2, 2:T + 2, :] = up.reshape(T, W, C)[:, 0:T, :]
    windows(gpad2, gs2, T + 4)
    load(3).wait()
    conv(gs2, w2, pg, 0, MP, True)
    pad_rims = hot(iota((4 * W, MP), 1) == rim_pos(iota((4 * W, 1), 0), T, 1))
    rims = dot(pad_rims, pg[...].astype(BF16)).astype(BF16)
    ex_start(2, recv_mat, recv_low, rims)
    gact[...] = pg[...].reshape(T + 2, W, C)[1:T + 1]
    pad_act[...] = jnp.zeros(pad_act.shape, F32)
    gpad1[...] = jnp.zeros(gpad1.shape, F32)
    for ph in range(4):
        ex_in[ph, sub] = jnp.zeros((W + LOW, LANES), BF16)
        ex_in[ph, pl.ds(S + 4 * face, 4)] = jnp.zeros((4, W + LOW, LANES), BF16)

    halo0 = ex_wait(0, recv_mat, recv_low)
    add_halo(pad_in, halo0)
    windows(pad_in, win_in, T + 2)
    load(5).wait()
    load(6).wait()
    conv(win_in, w1, hidden, 0, M, False)
    hid = hidden[...] + b1[...]
    sig = 1.0 / (1.0 + jnp.exp(-hid))
    act = (hid * sig).astype(BF16)
    rims = dot(own_rims, act).astype(BF16)
    ex_start(1, send_mat, send_low, rims)
    pad_act[1:T + 1, 1:T + 1, :] = act.astype(F32).reshape(T, W, C)[:, 0:T, :]
    slope = (sig * (1.0 + hid * (1.0 - sig))).reshape(T, W, C)[:, 0:T, :]

    def fold(middle, arrived):
        own_place = hot(iota((M, 4 * W), 0) == rim_pos(iota((1, 4 * W), 1), T, 0))
        hi, lo = split(arrived)
        back = dot(own_place, hi) + dot(own_place, lo)
        return middle[:, 1:T + 1, :] + back.reshape(T, W, C)[:, 0:T, :]

    halo2 = ex_wait(2, send_mat, send_low)
    ga = fold(gact, halo2).astype(BF16).astype(F32)
    gh = (ga * slope).astype(BF16).astype(F32)
    gpad1[2:T + 2, 2:T + 2, :] = gh
    windows(gpad1, gs1, T + 4)

    rows = wf.shape[1]

    def face_copy(k, f, f_in):
        return pltpu.make_async_remote_copy(
            src_ref=wb.at[k, pl.ds(pl.multiple_of(f * part, 16), part), :],
            dst_ref=w1in.at[k, f_in],
            send_sem=w_ss.at[k, 0], recv_sem=w_rs.at[k, 0],
            device_id=(f, sub), device_id_type=MESH)

    def b_copy(k, j, j_in):
        return pltpu.make_async_remote_copy(
            src_ref=red.at[k, pl.ds(pl.multiple_of(j * group, 16), group), :],
            dst_ref=w2in.at[k, j_in],
            send_sem=w_ss.at[k, 1], recv_sem=w_rs.at[k, 1],
            device_id=(face, a_id * B + j), device_id_type=MESH)

    def a_copy(k, j, j_in):
        return pltpu.make_async_remote_copy(
            src_ref=red2.at[k, pl.ds(pl.multiple_of(j * chunk, 16), chunk), :],
            dst_ref=w3in.at[k, j_in],
            send_sem=w_ss.at[k, 2], recv_sem=w_rs.at[k, 2],
            device_id=(face, j * B + b_id), device_id_type=MESH)

    def spot(k, start, size):
        return gath.at[k, pl.ds(pl.multiple_of(start, 16), size), :]

    def a_gather(k, j, own):
        place = spot(k, face * part + b_id * group + own * chunk, chunk)
        return pltpu.make_async_remote_copy(
            src_ref=place, dst_ref=place,
            send_sem=w_ss.at[k, 3], recv_sem=w_rs.at[k, 3],
            device_id=(face, j * B + b_id), device_id_type=MESH)

    def b_gather(k, j, own):
        place = spot(k, face * part + own * group, group)
        return pltpu.make_async_remote_copy(
            src_ref=place, dst_ref=place,
            send_sem=w_ss.at[k, 4], recv_sem=w_rs.at[k, 4],
            device_id=(face, a_id * B + j), device_id_type=MESH)

    def face_gather(k, f, own):
        place = spot(k, own * part, part)
        return pltpu.make_async_remote_copy(
            src_ref=place, dst_ref=place,
            send_sem=w_ss.at[k, 5], recv_sem=w_rs.at[k, 5],
            device_id=(f, sub), device_id_type=MESH)

    sizes = ((F - 1) * part, (B - 1) * group, (A - 1) * chunk, (A - 1) * chunk, (B - 1) * group, (F - 1) * part)

    counts = (F - 1, B - 1, A - 1)

    def arrived_all(k, st):
        if sizes[st]:
            slots = (w1in, w2in, w3in)
            take(slots[st].at[k, 0:counts[st]] if st < 3 else gath.at[k, 0:sizes[st], :], w_rs.at[k, st])

    def reduce_start(k):
        peers(F, face, lambda f: face_copy(k, f, face).start())

    def summed(first, count, mine, ref, k):
        def step(d, tot):
            return tot + ref[k, lax.rem(mine + d, count)].astype(F32)
        return lax.fori_loop(1, count, step, first)

    def reduce_b(k):
        arrived_all(k, 0)
        for r in range(B):
            at = pl.ds(pl.multiple_of(face * part + r * group, 16), group)
            tot = wf[k, at, :]
            for f in range(1, F):
                tot = tot + w1in[k, lax.rem(face + f, F), r * group:(r + 1) * group, :].astype(F32)
            accf[k, r * group:(r + 1) * group, :] = tot
            red[k, r * group:(r + 1) * group, :] = tot.astype(BF16)
        peers(B, b_id, lambda j: b_copy(k, j, b_id).start())

    def reduce_a(k):
        arrived_all(k, 1)
        tot = summed(accf[k, pl.ds(pl.multiple_of(b_id * group, 16), group), :], B, b_id, w2in, k)
        acc2[k] = tot
        red2[k] = tot.astype(BF16)
        peers(A, a_id, lambda j: a_copy(k, j, a_id).start())

    def gather_a(k):
        arrived_all(k, 2)
        tot = summed(acc2[k, pl.ds(pl.multiple_of(a_id * chunk, 16), chunk), :], A, a_id, w3in, k)
        own = pl.ds(pl.multiple_of(face * part + b_id * group + a_id * chunk, 16), chunk)
        gath[k, own, :] = (tot * scale).astype(BF16)
        peers(A, a_id, lambda j: a_gather(k, j, a_id).start())

    def gather_b(k):
        arrived_all(k, 3)
        peers(B, b_id, lambda j: b_gather(k, j, b_id).start())

    def gather_face(k):
        arrived_all(k, 4)
        peers(F, face, lambda f: face_gather(k, f, face).start())

    def gather_end(k):
        arrived_all(k, 5)

    def drain(k):
        for st in range(6):
            if sizes[st]:
                take((wb, red, red2, gath, gath, gath)[st].at[k, 0:sizes[st], :], w_ss.at[k, st])

    for k in range(2):
        put(k, 14 * C, jnp.zeros((rows - 14 * C, LANES), F32))
    weight_grad(0, win_in, gs1)
    bias = jnp.sum(jnp.sum(gh, axis=0), axis=0, keepdims=True)
    bias = jnp.concatenate([bias, jnp.zeros((1, 2 * LANES - C), F32)], axis=1)
    line = iota((16, LANES), 0)
    put(0, 14 * C, jnp.where(line == 0, bias[:, 0:LANES], jnp.where(line == 1, bias[:, LANES:], 0.0)))
    reduce_start(0)

    half = (T + 2) // 2 * W
    conv(gs1, w1, pg, 0, half, True)
    reduce_b(0)
    conv(gs1, w1, pg, half, MP - half, True)
    rims = dot(pad_rims, pg[...].astype(BF16)).astype(BF16)
    ex_start(3, recv_mat, recv_low, rims)
    halo1 = ex_wait(1, recv_mat, recv_low)
    add_halo(pad_act, halo1)
    windows(pad_act, win_act, T + 2)
    weight_grad(1, win_act, gs2)
    reduce_start(1)
    conv(win_act, w2, second, 0, M // 2, False)
    reduce_b(1)
    reduce_a(0)
    conv(win_act, w2, second, M // 2, M // 2, False)
    hi, lo = split(second[...] + pad_in[1:T + 1, 1:W + 1, :].reshape(M, C))
    mean = hot(pool_pos(iota((1, M), 1)) == iota((H * 16, M), 0))
    down = (dot(mean, hi) + dot(mean, lo)) * 0.25
    pooled[...] = down.reshape(H, 16, C)[:, 0:H, :].astype(BF16)
    gather_a(0)
    reduce_a(1)
    gact[...] = pg[...].reshape(T + 2, W, C)[1:T + 1]
    halo3 = ex_wait(3, send_mat, send_low)
    total = fold(gact, halo3) + gpad2[2:T + 2, 2:T + 2, :]
    gin[...] = total.astype(BF16)
    gather_b(0)
    gather_a(1)
    gather_b(1)
    gather_face(0)
    gather_face(1)
    gather_end(0)
    gather_end(1)
    for ph in range(4):
        ex_drain(ph)
    for k in range(2):
        drain(k)


def finish(C, pooled_in, gin_in, gath, pooled, gin, gw1, gb1, gw2):
    pooled[...] = pooled_in[...]
    gin[...] = gin_in[...]
    for k, out in ((0, gw1), (1, gw2)):
        for t in range(9):
            left = gath[k, t * C:(t + 1) * C, :].astype(F32)
            pair = gath[k, (9 + t // 2) * C:(10 + t // 2) * C, :].astype(F32)
            half = C - LANES
            right = pair[:, 0:half] if t % 2 == 0 else pair[:, half:2 * half]
            out[t // 3, t % 3, :, 0:LANES] = left
            out[t // 3, t % 3, :, LANES:C] = right
    bias = gath[0, 14 * C:14 * C + 16, :].astype(F32)
    gb1[:, 0:LANES] = bias[0:1]
    gb1[:, LANES:C] = bias[1:2, 0:C - LANES]


def local(S, F, features, w_first, b_first, w_second, neighbours, rotations, cotangent):
    T, C = features.shape[1], features.shape[2]
    H = T // 2
    D = neighbours.shape[0]
    chunk = -(-(14 * C + 16) // (16 * D)) * 16
    A = 4 if S % 4 == 0 else 1
    B = S // A
    rows, part = chunk * D, chunk * S
    K = S + 4 * F
    scale = 1.0 / math.sqrt(D * T * T)
    vm = pl.BlockSpec(memory_space=pltpu.VMEM)
    pooled, gin, gath = pl.pallas_call(
        functools.partial(kernel, S, F, chunk, scale),
        out_shape=(
            pltpu.VMEM((H, H, C), BF16),
            pltpu.VMEM((T, T, C), BF16),
            pltpu.VMEM((2, rows, LANES), BF16),
        ),
        in_specs=[pl.BlockSpec(memory_space=pl.ANY)] * 7,
        out_specs=(vm,) * 3,
        scratch_shapes=[
            pltpu.SMEM((4, D), jnp.int32),
            pltpu.SMEM((4, D), jnp.int32),
            pltpu.VMEM((T, T, C), BF16),
            pltpu.VMEM((H, H, C), BF16),
            pltpu.VMEM((9 * C, C), BF16),
            pltpu.VMEM((1, C), F32),
            pltpu.VMEM((9 * C, C), BF16),
            pltpu.VMEM((K * W, 4 * W), BF16),
            pltpu.VMEM((K * W, 4 * W), BF16),
            pltpu.VMEM((K * LOW, 8 * W), BF16),
            pltpu.VMEM((K * LOW, 8 * W), BF16),
            pltpu.VMEM((T + 2, W + 8, C), F32),
            pltpu.VMEM((T + 2, W + 8, C), F32),
            pltpu.VMEM((T + 4, W + 8, C), F32),
            pltpu.VMEM((T + 4, W + 8, C), F32),
            pltpu.VMEM((H, 16, C), F32),
            pltpu.VMEM((3, (T + 2) * W, C), BF16),
            pltpu.VMEM((3, (T + 2) * W, C), BF16),
            pltpu.VMEM((3, (T + 4) * W, C), BF16),
            pltpu.VMEM((3, (T + 4) * W, C), BF16),
            pltpu.VMEM((T * W, C), F32),
            pltpu.VMEM((T * W, C), F32),
            pltpu.VMEM(((T + 2) * W, C), F32),
            pltpu.VMEM((T, W, C), F32),
            pltpu.VMEM((4, K, W + LOW, LANES), BF16),
            pltpu.VMEM((4, K, W + LOW, LANES), BF16),
            pltpu.VMEM((2, rows, LANES), F32),
            pltpu.VMEM((2, rows, LANES), BF16),
            pltpu.VMEM((2, F, part, LANES), BF16),
            pltpu.VMEM((2, part, LANES), BF16),
            pltpu.VMEM((2, part, LANES), F32),
            pltpu.VMEM((2, B, A * chunk, LANES), BF16),
            pltpu.VMEM((2, A * chunk, LANES), BF16),
            pltpu.VMEM((2, A * chunk, LANES), F32),
            pltpu.VMEM((2, A, chunk, LANES), BF16),
            pltpu.SemaphoreType.DMA((4,)),
            pltpu.SemaphoreType.DMA((4,)),
            pltpu.SemaphoreType.DMA((2, 6)),
            pltpu.SemaphoreType.DMA((2, 6)),
            pltpu.SemaphoreType.DMA((7,)),
        ],
        compiler_params=pltpu.CompilerParams(
            collective_id=0, has_side_effects=True, vmem_limit_bytes=56 * 1024 * 1024
        ),
        name="level",
    )(
        neighbours.T, rotations.T, features, cotangent,
        w_first.reshape(9 * C, C), b_first.reshape(1, C), w_second.reshape(9 * C, C),
    )
    pooled, gin, gw1, gb1, gw2 = pl.pallas_call(
        functools.partial(finish, C),
        out_shape=(
            jax.ShapeDtypeStruct((H, H, C), BF16),
            jax.ShapeDtypeStruct((T, T, C), BF16),
            jax.ShapeDtypeStruct((3, 3, C, C), F32),
            jax.ShapeDtypeStruct((1, C), F32),
            jax.ShapeDtypeStruct((3, 3, C, C), F32),
        ),
        in_specs=[vm] * 3,
        out_specs=(vm,) * 5,
        compiler_params=pltpu.CompilerParams(vmem_limit_bytes=24 * 1024 * 1024),
        name="finish",
    )(pooled, gin, gath)
    return (pooled, gin, gw1, gb1.reshape(C), gw2)


def solution(mesh):
    tiles = P(("face", "sub"), None, None)
    return jax.shard_map(
        functools.partial(local, mesh.shape["sub"], mesh.shape["face"]),
        mesh=mesh,
        in_specs=(tiles, P(), P(), P(), P(), P(), tiles),
        out_specs=(tiles, tiles, P(), P(), P()),
        check_vma=False,
    )
```

```python
import functools
import math

import jax
import jax.numpy as jnp
from jax import lax
from jax.experimental import pallas as pl
from jax.experimental.pallas import tpu as pltpu
from jax.sharding import PartitionSpec as P

LANES = 128
W = 32
LOW = 16
PIECES = (5, 6)
F32, BF16 = jnp.float32, jnp.bfloat16
MESH = pl.DeviceIdType.MESH


def iota(shape, dim):
    return lax.broadcasted_iota(jnp.int32, shape, dim)


def hot(mask):
    return jnp.where(mask, 1.0, 0.0).astype(BF16)


def dot(a, b, ca=1, cb=0):
    return lax.dot_general(a, b, (((ca,), (cb,)), ((), ())), preferred_element_type=F32)


def split(x):
    hi = x.astype(BF16)
    return hi, (x - hi.astype(F32)).astype(BF16)


def rim_pos(q, extent, pad):
    e, p = q >> 5, (q & (W - 1)) + pad
    far = extent - 1 + 2 * pad
    pos = jnp.where(e == 0, p, jnp.where(e == 1, p * W + far, jnp.where(e == 2, far * W + p, p * W)))
    return jnp.where((q & (W - 1)) < extent, pos, -1)


def pool_pos(r):
    return ((r >> 6) << 4) + ((r & (W - 1)) >> 1)


def kernel(S, F, pieces, scale, nbr_hbm, rot_hbm, feat_hbm, cot_hbm, w1_hbm, b1_hbm, w2_hbm,
           pooled, gin, gath,
           nbr, rot, feat, cot, w1, b1, w2,
           send_mat, recv_mat, send_low, recv_low, pad_in, pad_act, gpad1, gpad2, cotp,
           win_in, win_act, gs1, gs2, hidden, second, pg, gact,
           ex_out, ex_in, wf, wb, w1in, red, accf, w2in, red2, acc2, w3in,
           ex_ss, ex_rs, w_ss, w_rs, in_sem):
    T, C = feat.shape[0], feat.shape[2]
    H = T // 2
    face, sub = lax.axis_index("face"), lax.axis_index("sub")
    me = face * S + sub
    A = 4 if S % 4 == 0 else 1
    B = S // A
    a_id, b_id = sub // B, lax.rem(sub, B)
    M, MP = T * W, (T + 2) * W

    def peers(count, mine, body):
        def step(d, c):
            body(lax.rem(mine + d, count))
            return c
        lax.fori_loop(1, count, step, 0)

    barrier = pltpu.get_barrier_semaphore()
    peers(S, sub, lambda j: pl.semaphore_signal(barrier, inc=1, device_id=(face, j), device_id_type=MESH))
    peers(F, face, lambda f: pl.semaphore_signal(barrier, inc=1, device_id=(f, sub), device_id_type=MESH))

    def load(i):
        pairs = ((nbr_hbm, nbr), (rot_hbm, rot), (feat_hbm, feat), (w2_hbm, w2), (cot_hbm, cot), (w1_hbm, w1), (b1_hbm, b1))
        return pltpu.make_async_copy(pairs[i][0], pairs[i][1], in_sem.at[i])

    for i in (2, 0, 1, 3, 4, 5, 6):
        load(i).start()

    p32 = iota((W, 4 * W), 0)
    c32 = iota((W, 4 * W), 1)

    q16 = iota((LOW, 8 * W), 0)
    d16 = iota((LOW, 8 * W), 1)
    low_pix = q16 + jnp.where(d16 >= 4 * W, H, 0)
    low_col = d16 & (4 * W - 1)

    def put_send(k, hit, src, flip):
        tgt = jnp.where(flip == 1, src * W + T - 1 - p32, src * W + p32)
        send_mat[pl.ds(pl.multiple_of(k * W, W), W), :] = hot((c32 == tgt) & (p32 < T) & (hit == 1))
        tgt = jnp.where(flip == 1, src * W + T - 1 - low_pix, src * W + low_pix)
        send_low[pl.ds(pl.multiple_of(k * LOW, LOW), LOW), :] = hot((low_col == tgt) & (q16 < H) & (hit == 1))

    def put_recv(k, edge):
        recv_mat[pl.ds(pl.multiple_of(k * W, W), W), :] = hot((c32 == edge * W + p32) & (p32 < T) & (edge >= 0))
        recv_low[pl.ds(pl.multiple_of(k * LOW, LOW), LOW), :] = hot(
            (low_col == edge * W + low_pix) & (q16 < H) & (edge >= 0))

    def edge_code(tile, e):
        r = rot[e, tile]
        x = (e + 2) % 4
        src = (x + r) & 3
        odd = x % 2
        flip = jnp.where(r == 2, 1, jnp.where(r == 1, odd, jnp.where(r == 3, 1 - odd, 0)))
        return nbr[e, tile] == me, src, flip

    def send_in_face(j, c):
        hit, src, flip = jnp.int32(0), jnp.int32(0), jnp.int32(0)
        for e in range(4):
            h, s, f = edge_code(face * S + j, e)
            hit = jnp.where(h, 1, hit)
            src = jnp.where(h, s, src)
            flip = jnp.where(h, f, flip)
        put_send(j, hit, src, flip)
        return c

    def send_cross(f, c):
        for e in range(4):
            h, s, fl = edge_code(f * S + sub, e)
            put_send(S + f * 4 + e, jnp.where(h & (f != face), 1, 0), s, fl)
        return c

    def recv_in_face(j, c):
        edge = jnp.int32(-1)
        for e in range(4):
            edge = jnp.where(nbr[e, me] == face * S + j, e, edge)
        put_recv(j, edge)
        return c

    def recv_cross(f, c):
        for e in range(4):
            put_recv(S + f * 4 + e, jnp.where((nbr[e, me] == f * S + sub) & (f != face), e, -1))
        return c

    def ex_sub(ph, j, s_in):
        return pltpu.make_async_remote_copy(
            src_ref=ex_out.at[ph, j], dst_ref=ex_in.at[ph, s_in],
            send_sem=ex_ss.at[ph], recv_sem=ex_rs.at[ph],
            device_id=(face, j), device_id_type=MESH)

    def ex_face(ph, f, f_in):
        return pltpu.make_async_remote_copy(
            src_ref=ex_out.at[ph, pl.ds(S + 4 * f, 4)], dst_ref=ex_in.at[ph, pl.ds(S + 4 * f_in, 4)],
            send_sem=ex_ss.at[ph], recv_sem=ex_rs.at[ph],
            device_id=(f, sub), device_id_type=MESH)

    slots = S + 4 * F
    R = C - LANES

    def ex_start(ph, mat, low, rims):
        zero = jnp.zeros((4 * W, R), BF16)
        wide = jnp.concatenate([
            jnp.concatenate([rims[:, LANES:C], zero], axis=1),
            jnp.concatenate([zero, rims[:, LANES:C]], axis=1)], axis=0)
        top = dot(mat[...], rims[:, 0:LANES]).reshape(slots, W, LANES)[:, 0:T, :]
        bottom = dot(low[...], wide).reshape(slots, LOW, LANES)
        ex_out[ph] = jnp.concatenate([top, bottom], axis=1).astype(BF16)
        peers(F, face, lambda f: ex_face(ph, f, face).start())
        peers(S, sub, lambda j: ex_sub(ph, j, sub).start())

    def take(ref, sem):
        pltpu.make_async_copy(ref, ref, sem).wait()

    ex_count = S - 1 + (F - 1) * 4

    def ex_wait(ph, mat, low):
        take(ex_in.at[ph, 0:ex_count], ex_rs.at[ph])
        got = ex_in[ph].astype(F32)
        left = dot(mat[...], got[:, 0:W, :].reshape(slots * W, LANES).astype(BF16), 0, 0)
        rest = dot(low[...], got[:, T:T + LOW, :].reshape(slots * LOW, LANES).astype(BF16), 0, 0)
        rest = rest[0:4 * W, 0:R] + rest[4 * W:8 * W, R:2 * R]
        return jnp.concatenate([left, rest], axis=1)

    def ex_drain(ph):
        take(ex_out.at[ph, 0:ex_count], ex_ss.at[ph])

    own_rims = hot(iota((4 * W, M), 1) == rim_pos(iota((4 * W, 1), 0), T, 0))

    def windows(src, dst, rows):
        for b in range(3):
            dst[b] = src[:, b:b + W, :].reshape(rows * W, C).astype(BF16)

    def add_halo(padded, halo):
        pad_place = hot(iota((MP, 4 * W), 0) == rim_pos(iota((1, 4 * W), 1), T, 1))
        placed = dot(pad_place, halo.astype(BF16)).reshape(T + 2, W, C)
        padded[:, 0:W, :] = padded[:, 0:W, :] + placed

    def conv(win, wt, out, lo, n, back):
        acc = None
        for a in range(3):
            for b in range(3):
                x = win[b, lo + a * W:lo + a * W + n, :]
                tap = (2 - a) * 3 + 2 - b if back else a * 3 + b
                d = dot(x, wt[tap * C:(tap + 1) * C, :], 1, 1 if back else 0)
                acc = d if acc is None else acc + d
        out[lo:lo + n, :] = acc

    def put(r, v):
        wf[r:r + v.shape[0], :] = v
        wb[r:r + v.shape[0], :] = v.astype(BF16)

    def weight_grad(base, win, gs):
        for t in range(9):
            a, b = t // 3, t % 3
            v = dot(win[b], gs[2, (2 - a) * W:(2 - a) * W + MP, :], 0, 0)
            at = base + t // 2 * 3 * C
            put(at + t % 2 * C, v[:, 0:LANES])
            rest = v[:, LANES:C]
            if t % 2 == 0:
                even = rest
            if t % 2 == 1:
                put(at + 2 * C, jnp.concatenate([even, rest], axis=1))
            if t == 8:
                put(at + C, jnp.concatenate([rest, rest], axis=1))

    pad_in[...] = jnp.zeros(pad_in.shape, F32)
    load(2).wait()
    pad_in[1:T + 1, 1:T + 1, :] = feat[...].astype(F32)
    flat_in = pad_in[1:T + 1, 1:W + 1, :].reshape(M, C)
    rims = dot(own_rims, flat_in.astype(BF16)).astype(BF16)
    load(0).wait()
    load(1).wait()
    lax.fori_loop(0, S, send_in_face, 0)
    lax.fori_loop(0, F, send_cross, 0)
    pl.semaphore_wait(barrier, S + F - 2)
    ex_start(0, send_mat, send_low, rims)

    lax.fori_loop(0, S, recv_in_face, 0)
    lax.fori_loop(0, F, recv_cross, 0)
    cotp[...] = jnp.zeros(cotp.shape, F32)
    load(4).wait()
    cotp[:, 0:H, :] = cot[...].astype(F32)
    spread = hot(pool_pos(iota((M, 1), 0)) == iota((M, H * 16), 1))
    up = dot(spread, cotp[...].reshape(H * 16, C).astype(BF16)) * 0.25
    gpad2[...] = jnp.zeros(gpad2.shape, F32)
    gpad2[2:T + 2, 2:T + 2, :] = up.reshape(T, W, C)[:, 0:T, :]
    windows(gpad2, gs2, T + 4)
    load(3).wait()
    conv(gs2, w2, pg, 0, MP, True)
    pad_rims = hot(iota((4 * W, MP), 1) == rim_pos(iota((4 * W, 1), 0), T, 1))
    rims = dot(pad_rims, pg[...].astype(BF16)).astype(BF16)
    ex_start(2, recv_mat, recv_low, rims)
    gact[...] = pg[...].reshape(T + 2, W, C)[1:T + 1]
    pad_act[...] = jnp.zeros(pad_act.shape, F32)
    gpad1[...] = jnp.zeros(gpad1.shape, F32)
    for ph in range(4):
        ex_in[ph, sub] = jnp.zeros((T + LOW, LANES), BF16)
        ex_in[ph, pl.ds(S + 4 * face, 4)] = jnp.zeros((4, T + LOW, LANES), BF16)

    halo0 = ex_wait(0, recv_mat, recv_low)
    add_halo(pad_in, halo0)
    windows(pad_in, win_in, T + 2)
    load(5).wait()
    load(6).wait()
    conv(win_in, w1, hidden, 0, M, False)
    hid = hidden[...] + b1[...]
    sig = 1.0 / (1.0 + jnp.exp(-hid))
    act = (hid * sig).astype(BF16)
    rims = dot(own_rims, act).astype(BF16)
    ex_start(1, send_mat, send_low, rims)
    pad_act[1:T + 1, 1:T + 1, :] = act.astype(F32).reshape(T, W, C)[:, 0:T, :]
    slope = (sig * (1.0 + hid * (1.0 - sig))).reshape(T, W, C)[:, 0:T, :]

    def fold(middle, arrived):
        own_place = hot(iota((M, 4 * W), 0) == rim_pos(iota((1, 4 * W), 1), T, 0))
        hi, lo = split(arrived)
        back = dot(own_place, hi) + dot(own_place, lo)
        return middle[:, 1:T + 1, :] + back.reshape(T, W, C)[:, 0:T, :]

    halo2 = ex_wait(2, send_mat, send_low)
    ga = fold(gact, halo2).astype(BF16).astype(F32)
    gh = (ga * slope).astype(BF16).astype(F32)
    gpad1[2:T + 2, 2:T + 2, :] = gh
    windows(gpad1, gs1, T + 4)

    D = S * F
    starts = [sum(pieces[:p]) for p in range(len(pieces))]

    def whole(p, level):
        share = (D // F, D // (F * B), 1)[level]
        lo = starts[p] // D * share
        return slice(lo, lo + pieces[p] // D * share)

    def spot(ref, p, start, size):
        return ref.at[pl.ds(pl.multiple_of(starts[p] + start, 16), size), :]

    def sizes(p):
        chunk = pieces[p] // D
        return chunk * S, chunk * A, chunk

    def remote(p, st, src, dst, device):
        return pltpu.make_async_remote_copy(
            src_ref=src, dst_ref=dst, send_sem=w_ss.at[p, st], recv_sem=w_rs.at[p, st],
            device_id=device, device_id_type=MESH)

    def to_face(f):
        return (f, sub)

    def to_b(j):
        return (face, a_id * B + j)

    def to_a(j):
        return (face, j * B + b_id)

    def inner(p, level, start, ref):
        size = sizes(p)[level]
        base = starts[p] // D * (D // F, D // (F * B), 1)[level - 1]
        return ref.at[pl.ds(pl.multiple_of(base + start * size, 16), size), :]

    def face_copy(p, f, f_in):
        part = sizes(p)[0]
        return remote(p, 0, spot(wb, p, f * part, part), w1in.at[f_in, whole(p, 0)], to_face(f))

    def b_copy(p, j, j_in):
        return remote(p, 1, inner(p, 1, j, red), w2in.at[j_in, whole(p, 1)], to_b(j))

    def a_copy(p, j, j_in):
        return remote(p, 2, inner(p, 2, j, red2), w3in.at[j_in, whole(p, 2)], to_a(j))

    def a_gather(p, j, own):
        part, group, chunk = sizes(p)
        place = spot(gath, p, face * part + b_id * group + own * chunk, chunk)
        return remote(p, 3, place, place, to_a(j))

    def b_gather(p, j, own):
        part, group, chunk = sizes(p)
        place = spot(gath, p, face * part + own * group, group)
        return remote(p, 4, place, place, to_b(j))

    def face_gather(p, f, own):
        part, group, chunk = sizes(p)
        place = spot(gath, p, own * part, part)
        return remote(p, 5, place, place, to_face(f))

    counts = (F - 1, B - 1, A - 1, A - 1, B - 1, F - 1)

    def moved(p, st):
        return counts[st] * sizes(p)[(0, 1, 2, 2, 1, 0)[st]]

    def arrived_all(p, st):
        if counts[st]:
            if st < 3:
                take((w1in, w2in, w3in)[st].at[0:counts[st], whole(p, st)], w_rs.at[p, st])
            else:
                take(gath.at[starts[p]:starts[p] + moved(p, st), :], w_rs.at[p, st])

    def reduce_start(p):
        peers(F, face, lambda f: face_copy(p, f, face).start())

    def summed(first, count, mine, ref, span):
        def step(d, tot):
            return tot + ref[lax.rem(mine + d, count), span, :].astype(F32)
        return lax.fori_loop(1, count, step, first)

    def reduce_b(p):
        arrived_all(p, 0)
        part, group, chunk = sizes(p)
        lo = starts[p] // F
        for r in range(B):
            tot = wf[pl.ds(pl.multiple_of(starts[p] + face * part + r * group, 16), group), :]
            for f in range(1, F):
                tot = tot + w1in[lax.rem(face + f, F), lo + r * group:lo + (r + 1) * group, :].astype(F32)
            accf[lo + r * group:lo + (r + 1) * group, :] = tot
            red[lo + r * group:lo + (r + 1) * group, :] = tot.astype(BF16)
        peers(B, b_id, lambda j: b_copy(p, j, b_id).start())

    def reduce_a(p):
        arrived_all(p, 1)
        part, group, chunk = sizes(p)
        own = pl.ds(pl.multiple_of(starts[p] // F + b_id * group, 16), group)
        tot = summed(accf[own, :], B, b_id, w2in, whole(p, 1))
        acc2[whole(p, 1), :] = tot
        red2[whole(p, 1), :] = tot.astype(BF16)
        peers(A, a_id, lambda j: a_copy(p, j, a_id).start())

    def gather_a(p):
        arrived_all(p, 2)
        part, group, chunk = sizes(p)
        own = pl.ds(pl.multiple_of(starts[p] // (F * B) + a_id * chunk, 16), chunk)
        tot = summed(acc2[own, :], A, a_id, w3in, whole(p, 2))
        own = pl.ds(pl.multiple_of(starts[p] + face * part + b_id * group + a_id * chunk, 16), chunk)
        gath[own, :] = (tot * scale).astype(BF16)
        peers(A, a_id, lambda j: a_gather(p, j, a_id).start())

    def gather_b(p):
        arrived_all(p, 3)
        peers(B, b_id, lambda j: b_gather(p, j, b_id).start())

    def gather_face(p):
        arrived_all(p, 4)
        peers(F, face, lambda f: face_gather(p, f, face).start())

    def gather_end(p):
        arrived_all(p, 5)

    def drain(p):
        for st in range(6):
            if counts[st]:
                lo = starts[p] // (1, F, F * B, 1, 1, 1)[st]
                take((wb, red, red2, gath, gath, gath)[st].at[lo:lo + moved(p, st), :], w_ss.at[p, st])

    lines = 14 * C
    second_at = max(lines + 16, starts[1])
    used = second_at + lines
    put(used, jnp.zeros((wf.shape[0] - used, LANES), F32)) if wf.shape[0] > used else None
    put(lines + 16, jnp.zeros((second_at - lines - 16, LANES), F32)) if second_at > lines + 16 else None
    early = [p for p in range(len(pieces)) if starts[p] + pieces[p] <= second_at]
    late = [p for p in range(len(pieces)) if p not in early]
    weight_grad(0, win_in, gs1)
    bias = jnp.sum(jnp.sum(gh, axis=0), axis=0, keepdims=True)
    bias = jnp.concatenate([bias, jnp.zeros((1, 2 * LANES - C), F32)], axis=1)
    line = iota((16, LANES), 0)
    put(lines, jnp.where(line == 0, bias[:, 0:LANES], jnp.where(line == 1, bias[:, LANES:], 0.0)))
    for p in early:
        reduce_start(p)

    half = (T + 2) // 2 * W
    conv(gs1, w1, pg, 0, half, True)
    for p in early:
        reduce_b(p)
    halo1 = ex_wait(1, recv_mat, recv_low)
    add_halo(pad_act, halo1)
    windows(pad_act, win_act, T + 2)
    weight_grad(second_at, win_act, gs2)
    for p in late:
        reduce_start(p)
    conv(win_act, w2, second, 0, M // 2, False)
    reduce_b(1)
    reduce_a(0)
    conv(win_act, w2, second, M // 2, M // 2, False)
    gather_a(0)
    conv(gs1, w1, pg, half, MP - half, True)
    rims = dot(pad_rims, pg[...].astype(BF16)).astype(BF16)
    gact[...] = pg[...].reshape(T + 2, W, C)[1:T + 1]
    reduce_a(1)
    hi, lo = split(second[...] + pad_in[1:T + 1, 1:W + 1, :].reshape(M, C))
    mean = hot(pool_pos(iota((1, M), 1)) == iota((H * 16, M), 0))
    down = (dot(mean, hi) + dot(mean, lo)) * 0.25
    pooled[...] = down.reshape(H, 16, C)[:, 0:H, :].astype(BF16)
    gather_b(0)
    gather_a(1)
    ex_start(3, recv_mat, recv_low, rims)
    gather_b(1)
    gather_face(0)
    halo3 = ex_wait(3, send_mat, send_low)
    total = fold(gact, halo3) + gpad2[2:T + 2, 2:T + 2, :]
    gin[...] = total.astype(BF16)
    gather_face(1)
    gather_end(0)
    gather_end(1)
    for ph in range(4):
        ex_drain(ph)
    for p in range(len(pieces)):
        drain(p)


def finish(C, second_at, pooled_in, gin_in, gath, pooled, gin, gw1, gb1, gw2):
    pooled[...] = pooled_in[...]
    gin[...] = gin_in[...]
    for base, out in ((0, gw1), (second_at, gw2)):
        for t in range(9):
            lo = base + t // 2 * 3 * C
            left = gath[lo + t % 2 * C:lo + t % 2 * C + C, :].astype(F32)
            lo = lo + (2 * C if t < 8 else C)
            pair = gath[lo:lo + C, :].astype(F32)
            half = C - LANES
            right = pair[:, 0:half] if t % 2 == 0 else pair[:, half:2 * half]
            out[t // 3, t % 3, :, 0:LANES] = left
            out[t // 3, t % 3, :, LANES:C] = right
    bias = gath[14 * C:14 * C + 16, :].astype(F32)
    gb1[:, 0:LANES] = bias[0:1]
    gb1[:, LANES:C] = bias[1:2, 0:C - LANES]


def local(S, F, features, w_first, b_first, w_second, neighbours, rotations, cotangent):
    T, C = features.shape[1], features.shape[2]
    H = T // 2
    D = neighbours.shape[0]
    unit = 16 * D
    total = -(-(28 * C + 16) // unit)
    first = (14 * C + 16) // unit
    rest = total - first
    units = PIECES if D == 32 else ((first, rest) if first else (1, -(-14 * C // unit)))
    pieces = tuple(u * unit for u in units)
    A = 4 if S % 4 == 0 else 1
    B = S // A
    rows = sum(pieces)
    K = S + 4 * F
    scale = 1.0 / math.sqrt(D * T * T)
    vm = pl.BlockSpec(memory_space=pltpu.VMEM)
    pooled, gin, gath = pl.pallas_call(
        functools.partial(kernel, S, F, pieces, scale),
        out_shape=(
            pltpu.VMEM((H, H, C), BF16),
            pltpu.VMEM((T, T, C), BF16),
            pltpu.VMEM((rows, LANES), BF16),
        ),
        in_specs=[pl.BlockSpec(memory_space=pl.ANY)] * 7,
        out_specs=(vm,) * 3,
        scratch_shapes=[
            pltpu.SMEM((4, D), jnp.int32),
            pltpu.SMEM((4, D), jnp.int32),
            pltpu.VMEM((T, T, C), BF16),
            pltpu.VMEM((H, H, C), BF16),
            pltpu.VMEM((9 * C, C), BF16),
            pltpu.VMEM((1, C), F32),
            pltpu.VMEM((9 * C, C), BF16),
            pltpu.VMEM((K * W, 4 * W), BF16),
            pltpu.VMEM((K * W, 4 * W), BF16),
            pltpu.VMEM((K * LOW, 8 * W), BF16),
            pltpu.VMEM((K * LOW, 8 * W), BF16),
            pltpu.VMEM((T + 2, W + 8, C), F32),
            pltpu.VMEM((T + 2, W + 8, C), F32),
            pltpu.VMEM((T + 4, W + 8, C), F32),
            pltpu.VMEM((T + 4, W + 8, C), F32),
            pltpu.VMEM((H, 16, C), F32),
            pltpu.VMEM((3, (T + 2) * W, C), BF16),
            pltpu.VMEM((3, (T + 2) * W, C), BF16),
            pltpu.VMEM((3, (T + 4) * W, C), BF16),
            pltpu.VMEM((3, (T + 4) * W, C), BF16),
            pltpu.VMEM((T * W, C), F32),
            pltpu.VMEM((T * W, C), F32),
            pltpu.VMEM(((T + 2) * W, C), F32),
            pltpu.VMEM((T, W, C), F32),
            pltpu.VMEM((4, K, T + LOW, LANES), BF16),
            pltpu.VMEM((4, K, T + LOW, LANES), BF16),
            pltpu.VMEM((rows, LANES), F32),
            pltpu.VMEM((rows, LANES), BF16),
            pltpu.VMEM((F, rows // F, LANES), BF16),
            pltpu.VMEM((rows // F, LANES), BF16),
            pltpu.VMEM((rows // F, LANES), F32),
            pltpu.VMEM((B, rows // (F * B), LANES), BF16),
            pltpu.VMEM((rows // (F * B), LANES), BF16),
            pltpu.VMEM((rows // (F * B), LANES), F32),
            pltpu.VMEM((A, rows // D, LANES), BF16),
            pltpu.SemaphoreType.DMA((4,)),
            pltpu.SemaphoreType.DMA((4,)),
            pltpu.SemaphoreType.DMA((len(pieces), 6)),
            pltpu.SemaphoreType.DMA((len(pieces), 6)),
            pltpu.SemaphoreType.DMA((7,)),
        ],
        compiler_params=pltpu.CompilerParams(
            collective_id=0, has_side_effects=True, vmem_limit_bytes=56 * 1024 * 1024
        ),
        name="level",
    )(
        neighbours.T, rotations.T, features, cotangent,
        w_first.reshape(9 * C, C), b_first.reshape(1, C), w_second.reshape(9 * C, C),
    )
    pooled, gin, gw1, gb1, gw2 = pl.pallas_call(
        functools.partial(finish, C, max(14 * C + 16, pieces[0])),
        out_shape=(
            jax.ShapeDtypeStruct((H, H, C), BF16),
            jax.ShapeDtypeStruct((T, T, C), BF16),
            jax.ShapeDtypeStruct((3, 3, C, C), F32),
            jax.ShapeDtypeStruct((1, C), F32),
            jax.ShapeDtypeStruct((3, 3, C, C), F32),
        ),
        in_specs=[vm] * 3,
        out_specs=(vm,) * 5,
        compiler_params=pltpu.CompilerParams(vmem_limit_bytes=24 * 1024 * 1024),
        name="finish",
    )(pooled, gin, gath)
    return (pooled, gin, gw1, gb1.reshape(C), gw2)


def solution(mesh):
    tiles = P(("face", "sub"), None, None)
    return jax.shard_map(
        functools.partial(local, mesh.shape["sub"], mesh.shape["face"]),
        mesh=mesh,
        in_specs=(tiles, P(), P(), P(), P(), P(), tiles),
        out_specs=(tiles, tiles, P(), P(), P()),
        check_vma=False,
    )
```

```python
import functools
import math

import jax
import jax.numpy as jnp
from jax import lax
from jax.experimental import pallas as pl
from jax.experimental.pallas import tpu as pltpu
from jax.sharding import PartitionSpec as P

LANES = 128
W = 32
LOW = 16
F32, BF16 = jnp.float32, jnp.bfloat16
MESH = pl.DeviceIdType.MESH


def iota(shape, dim):
    return lax.broadcasted_iota(jnp.int32, shape, dim)


def hot(mask):
    return jnp.where(mask, 1.0, 0.0).astype(BF16)


def dot(a, b, ca=1, cb=0):
    return lax.dot_general(a, b, (((ca,), (cb,)), ((), ())), preferred_element_type=F32)


def split(x):
    hi = x.astype(BF16)
    return hi, (x - hi.astype(F32)).astype(BF16)


def rim_pos(q, extent, pad):
    e, p = q >> 5, (q & (W - 1)) + pad
    far = extent - 1 + 2 * pad
    pos = jnp.where(e == 0, p, jnp.where(e == 1, p * W + far, jnp.where(e == 2, far * W + p, p * W)))
    return jnp.where((q & (W - 1)) < extent, pos, -1)


def pool_pos(r):
    return ((r >> 6) << 4) + ((r & (W - 1)) >> 1)


def kernel(S, F, pieces, scale, nbr_hbm, rot_hbm, feat_hbm, cot_hbm, w1_hbm, b1_hbm, w2_hbm,
           pooled, gin, gath,
           nbr, rot, feat, cot, w1, b1, w2,
           send_mat, recv_mat, send_low, recv_low, pad_in, pad_act, gpad1, gpad2, cotp,
           win_in, win_act, gs1, gs2, hidden, second, pg, gact,
           ex_out, ex_in, wf, wb, w1in, red, accf, w2in, red2, w3in,
           ex_ss, ex_rs, w_ss, w_rs, in_sem):
    T, C = feat.shape[0], feat.shape[2]
    H = T // 2
    face, sub = lax.axis_index("face"), lax.axis_index("sub")
    me = face * S + sub
    A = 2 if S % 2 == 0 else 1
    B = S // A
    a_id, b_id = sub // B, lax.rem(sub, B)
    M, MP = T * W, (T + 2) * W

    def peers(count, mine, body):
        def step(d, c):
            body(lax.rem(mine + d, count))
            return c
        lax.fori_loop(1, count, step, 0)

    def load(i):
        pairs = ((nbr_hbm, nbr), (rot_hbm, rot), (feat_hbm, feat), (w2_hbm, w2), (cot_hbm, cot), (w1_hbm, w1), (b1_hbm, b1))
        return pltpu.make_async_copy(pairs[i][0], pairs[i][1], in_sem.at[i])

    for i in (2, 0, 1, 3, 4, 5, 6):
        load(i).start()

    barrier = pltpu.get_barrier_semaphore()
    peers(S, sub, lambda j: pl.semaphore_signal(barrier, inc=1, device_id=(face, j), device_id_type=MESH))
    peers(F, face, lambda f: pl.semaphore_signal(barrier, inc=1, device_id=(f, sub), device_id_type=MESH))

    p32 = iota((W, 4 * W), 0)
    c32 = iota((W, 4 * W), 1)

    q16 = iota((LOW, 8 * W), 0)
    d16 = iota((LOW, 8 * W), 1)
    low_pix = q16 + jnp.where(d16 >= 4 * W, H, 0)
    low_col = d16 & (4 * W - 1)

    def put_send(k, hit, src, flip):
        tgt = jnp.where(flip == 1, src * W + T - 1 - p32, src * W + p32)
        send_mat[pl.ds(pl.multiple_of(k * W, W), W), :] = hot((c32 == tgt) & (p32 < T) & (hit == 1))
        tgt = jnp.where(flip == 1, src * W + T - 1 - low_pix, src * W + low_pix)
        send_low[pl.ds(pl.multiple_of(k * LOW, LOW), LOW), :] = hot((low_col == tgt) & (q16 < H) & (hit == 1))

    def put_recv(k, edge):
        recv_mat[pl.ds(pl.multiple_of(k * W, W), W), :] = hot((c32 == edge * W + p32) & (p32 < T) & (edge >= 0))
        recv_low[pl.ds(pl.multiple_of(k * LOW, LOW), LOW), :] = hot(
            (low_col == edge * W + low_pix) & (q16 < H) & (edge >= 0))

    def edge_code(tile, e):
        r = rot[e, tile]
        x = (e + 2) % 4
        src = (x + r) & 3
        odd = x % 2
        flip = jnp.where(r == 2, 1, jnp.where(r == 1, odd, jnp.where(r == 3, 1 - odd, 0)))
        return nbr[e, tile] == me, src, flip

    def send_in_face(j, c):
        hit, src, flip = jnp.int32(0), jnp.int32(0), jnp.int32(0)
        for e in range(4):
            h, s, f = edge_code(face * S + j, e)
            hit = jnp.where(h, 1, hit)
            src = jnp.where(h, s, src)
            flip = jnp.where(h, f, flip)
        put_send(j, hit, src, flip)
        return c

    def send_cross(f, c):
        for e in range(4):
            h, s, fl = edge_code(f * S + sub, e)
            put_send(S + f * 4 + e, jnp.where(h & (f != face), 1, 0), s, fl)
        return c

    def recv_in_face(j, c):
        edge = jnp.int32(-1)
        for e in range(4):
            edge = jnp.where(nbr[e, me] == face * S + j, e, edge)
        put_recv(j, edge)
        return c

    def recv_cross(f, c):
        for e in range(4):
            put_recv(S + f * 4 + e, jnp.where((nbr[e, me] == f * S + sub) & (f != face), e, -1))
        return c

    def ex_sub(ph, j, s_in):
        return pltpu.make_async_remote_copy(
            src_ref=ex_out.at[ph, j], dst_ref=ex_in.at[ph, s_in],
            send_sem=ex_ss.at[ph], recv_sem=ex_rs.at[ph],
            device_id=(face, j), device_id_type=MESH)

    def ex_face(ph, f, f_in):
        return pltpu.make_async_remote_copy(
            src_ref=ex_out.at[ph, pl.ds(S + 4 * f, 4)], dst_ref=ex_in.at[ph, pl.ds(S + 4 * f_in, 4)],
            send_sem=ex_ss.at[ph], recv_sem=ex_rs.at[ph],
            device_id=(f, sub), device_id_type=MESH)

    slots = S + 4 * F
    R = C - LANES

    def ex_start(ph, mat, low, rims):
        zero = jnp.zeros((4 * W, R), BF16)
        wide = jnp.concatenate([
            jnp.concatenate([rims[:, LANES:C], zero], axis=1),
            jnp.concatenate([zero, rims[:, LANES:C]], axis=1)], axis=0)
        top = dot(mat[...], rims[:, 0:LANES]).reshape(slots, W, LANES)[:, 0:T, :]
        bottom = dot(low[...], wide).reshape(slots, LOW, LANES)
        ex_out[ph] = jnp.concatenate([top, bottom], axis=1).astype(BF16)
        peers(F, face, lambda f: ex_face(ph, f, face).start())
        peers(S, sub, lambda j: ex_sub(ph, j, sub).start())

    def take(ref, sem):
        pltpu.make_async_copy(ref, ref, sem).wait()

    ex_count = S - 1 + (F - 1) * 4

    def ex_wait(ph, mat, low):
        take(ex_in.at[ph, 0:ex_count], ex_rs.at[ph])
        got = ex_in[ph].astype(F32)
        left = dot(mat[...], got[:, 0:W, :].reshape(slots * W, LANES).astype(BF16), 0, 0)
        rest = dot(low[...], got[:, T:T + LOW, :].reshape(slots * LOW, LANES).astype(BF16), 0, 0)
        rest = rest[0:4 * W, 0:R] + rest[4 * W:8 * W, R:2 * R]
        return jnp.concatenate([left, rest], axis=1)

    def ex_drain(ph):
        take(ex_out.at[ph, 0:ex_count], ex_ss.at[ph])


    def windows(src, dst, rows):
        for b in range(3):
            dst[b] = src[:, b:b + W, :].reshape(rows * W, C).astype(BF16)

    def add_halo(padded, halo):
        pad_place = hot(iota((MP, 4 * W), 0) == rim_pos(iota((1, 4 * W), 1), T, 1))
        placed = dot(pad_place, halo.astype(BF16)).reshape(T + 2, W, C)
        padded[:, 0:W, :] = padded[:, 0:W, :] + placed

    def conv(win, wt, out, lo, n, back):
        acc = None
        for a in range(3):
            for b in range(3):
                x = win[b, lo + a * W:lo + a * W + n, :]
                tap = (2 - a) * 3 + 2 - b if back else a * 3 + b
                d = dot(x, wt[tap * C:(tap + 1) * C, :], 1, 1 if back else 0)
                acc = d if acc is None else acc + d
        out[lo:lo + n, :] = acc

    def put(r, v):
        wf[r:r + v.shape[0], :] = v
        wb[r:r + v.shape[0], :] = v.astype(BF16)

    def weight_grad(base, win, gs, spare):
        for t in range(9):
            a, b = t // 3, t % 3
            v = dot(win[b], gs[2, (2 - a) * W:(2 - a) * W + MP, :], 0, 0)
            at = base + t // 2 * 3 * C
            put(at + t % 2 * C, v[:, 0:LANES])
            rest = v[:, LANES:C]
            if t % 2 == 0:
                even = rest
            if t % 2 == 1:
                put(at + 2 * C, jnp.concatenate([even, rest], axis=1))
            if t == 8:
                put(at + C, jnp.concatenate([rest, spare], axis=1))

    pad_in[...] = jnp.zeros(pad_in.shape, F32)
    load(0).wait()
    load(1).wait()
    lax.fori_loop(0, S, send_in_face, 0)
    lax.fori_loop(0, F, send_cross, 0)
    own_rims = hot(iota((4 * W, M), 1) == rim_pos(iota((4 * W, 1), 0), T, 0))
    load(2).wait()
    pad_in[1:T + 1, 1:T + 1, :] = feat[...].astype(F32)
    flat_in = pad_in[1:T + 1, 1:W + 1, :].reshape(M, C)
    rims = dot(own_rims, flat_in.astype(BF16)).astype(BF16)
    pl.semaphore_wait(barrier, S + F - 2)
    ex_start(0, send_mat, send_low, rims)

    lax.fori_loop(0, S, recv_in_face, 0)
    lax.fori_loop(0, F, recv_cross, 0)
    cotp[...] = jnp.zeros(cotp.shape, F32)
    load(4).wait()
    cotp[:, 0:H, :] = cot[...].astype(F32)
    spread = hot(pool_pos(iota((M, 1), 0)) == iota((M, H * 16), 1))
    up = dot(spread, cotp[...].reshape(H * 16, C).astype(BF16)) * 0.25
    gpad2[...] = jnp.zeros(gpad2.shape, F32)
    gpad2[2:T + 2, 2:T + 2, :] = up.reshape(T, W, C)[:, 0:T, :]
    windows(gpad2, gs2, T + 4)
    load(3).wait()
    conv(gs2, w2, pg, 0, MP, True)
    pad_rims = hot(iota((4 * W, MP), 1) == rim_pos(iota((4 * W, 1), 0), T, 1))
    rims = dot(pad_rims, pg[...].astype(BF16)).astype(BF16)
    ex_start(2, recv_mat, recv_low, rims)
    gact[...] = pg[...].reshape(T + 2, W, C)[1:T + 1]
    pad_act[...] = jnp.zeros(pad_act.shape, F32)
    gpad1[...] = jnp.zeros(gpad1.shape, F32)
    for ph in range(4):
        ex_in[ph, sub] = jnp.zeros((T + LOW, LANES), BF16)
        ex_in[ph, pl.ds(S + 4 * face, 4)] = jnp.zeros((4, T + LOW, LANES), BF16)

    halo0 = ex_wait(0, recv_mat, recv_low)
    add_halo(pad_in, halo0)
    windows(pad_in, win_in, T + 2)
    load(5).wait()
    load(6).wait()
    conv(win_in, w1, hidden, 0, M, False)
    hid = hidden[...] + b1[...]
    sig = 1.0 / (1.0 + jnp.exp(-hid))
    act = (hid * sig).astype(BF16)
    rims = dot(own_rims, act).astype(BF16)
    ex_start(1, send_mat, send_low, rims)
    pad_act[1:T + 1, 1:T + 1, :] = act.astype(F32).reshape(T, W, C)[:, 0:T, :]
    slope = (sig * (1.0 + hid * (1.0 - sig))).reshape(T, W, C)[:, 0:T, :]

    def fold(middle, arrived):
        own_place = hot(iota((M, 4 * W), 0) == rim_pos(iota((1, 4 * W), 1), T, 0))
        hi, lo = split(arrived)
        back = dot(own_place, hi) + dot(own_place, lo)
        return middle[:, 1:T + 1, :] + back.reshape(T, W, C)[:, 0:T, :]

    halo2 = ex_wait(2, send_mat, send_low)
    ga = fold(gact, halo2).astype(BF16).astype(F32)
    gh = (ga * slope).astype(BF16).astype(F32)
    gpad1[2:T + 2, 2:T + 2, :] = gh
    windows(gpad1, gs1, T + 4)

    D = S * F
    starts = [sum(pieces[:p]) for p in range(len(pieces))]

    def whole(p, level):
        share = F if level == 0 else F * B
        return slice(starts[p] // share, (starts[p] + pieces[p]) // share)

    def spot(ref, p, start, size):
        return ref.at[pl.ds(pl.multiple_of(starts[p] + start, 16), size), :]

    def sizes(p):
        return pieces[p] // F, pieces[p] // (F * B)

    def remote(p, st, src, dst, device):
        return pltpu.make_async_remote_copy(
            src_ref=src, dst_ref=dst, send_sem=w_ss.at[p, st], recv_sem=w_rs.at[p, st],
            device_id=device, device_id_type=MESH)

    def to_face(f):
        return (f, sub)

    def to_b(j):
        return (face, a_id * B + j)

    def to_a(j):
        return (face, j * B + b_id)

    def face_copy(p, f, f_in):
        part = sizes(p)[0]
        return remote(p, 0, spot(wb, p, f * part, part), w1in.at[f_in, whole(p, 0)], to_face(f))

    def b_copy(p, j, j_in):
        group = sizes(p)[1]
        at = pl.ds(pl.multiple_of(starts[p] // F + j * group, 16), group)
        return remote(p, 1, red.at[at, :], w2in.at[j_in, whole(p, 1)], to_b(j))

    def a_copy(p, j, j_in):
        return remote(p, 2, red2.at[whole(p, 1)], w3in.at[j_in, whole(p, 1)], to_a(j))

    def b_gather(p, j, own):
        part, group = sizes(p)
        place = spot(gath, p, face * part + own * group, group)
        return remote(p, 3, place, place, to_b(j))

    def face_gather(p, f, own):
        part = sizes(p)[0]
        place = spot(gath, p, own * part, part)
        return remote(p, 4, place, place, to_face(f))

    counts = (F - 1, B - 1, A - 1, B - 1, F - 1)

    def moved(p, st):
        return counts[st] * sizes(p)[(0, 1, 1, 1, 0)[st]]

    def arrived_all(p, st):
        if counts[st]:
            if st < 3:
                take((w1in, w2in, w3in)[st].at[0:counts[st], whole(p, st)], w_rs.at[p, st])
            else:
                take(gath.at[starts[p]:starts[p] + moved(p, st), :], w_rs.at[p, st])

    def reduce_start(p):
        peers(F, face, lambda f: face_copy(p, f, face).start())

    def summed(first, count, mine, ref, span):
        def step(d, tot):
            return tot + ref[lax.rem(mine + d, count), span, :].astype(F32)
        return lax.fori_loop(1, count, step, first)

    def reduce_b(p):
        arrived_all(p, 0)
        part, group = sizes(p)
        lo = starts[p] // F
        for r in range(B):
            tot = wf[pl.ds(pl.multiple_of(starts[p] + face * part + r * group, 16), group), :]
            for f in range(1, F):
                tot = tot + w1in[lax.rem(face + f, F), lo + r * group:lo + (r + 1) * group, :].astype(F32)
            accf[lo + r * group:lo + (r + 1) * group, :] = tot
            red[lo + r * group:lo + (r + 1) * group, :] = tot.astype(BF16)
        peers(B, b_id, lambda j: b_copy(p, j, b_id).start())

    def reduce_a(p):
        arrived_all(p, 1)
        group = sizes(p)[1]
        own = pl.ds(pl.multiple_of(starts[p] // F + b_id * group, 16), group)
        tot = summed(accf[own, :], B, b_id, w2in, whole(p, 1))
        red2[whole(p, 1), :] = tot.astype(BF16)
        peers(A, a_id, lambda j: a_copy(p, j, a_id).start())

    def gather_b(p):
        arrived_all(p, 2)
        part, group = sizes(p)
        tot = summed(red2[whole(p, 1), :].astype(F32), A, a_id, w3in, whole(p, 1))
        own = pl.ds(pl.multiple_of(starts[p] + face * part + b_id * group, 16), group)
        gath[own, :] = (tot * scale).astype(BF16)
        peers(B, b_id, lambda j: b_gather(p, j, b_id).start())

    def gather_face(p):
        arrived_all(p, 3)
        peers(F, face, lambda f: face_gather(p, f, face).start())

    def gather_end(p):
        arrived_all(p, 4)

    def drain(p):
        for st in range(5):
            if counts[st]:
                lo = starts[p] // (1, F, F * B, 1, 1)[st]
                take((wb, red, red2, gath, gath)[st].at[lo:lo + moved(p, st), :], w_ss.at[p, st])

    lines = 14 * C
    second_at = max(lines, starts[1])
    used = second_at + lines
    if wf.shape[0] > used:
        put(used, jnp.zeros((wf.shape[0] - used, LANES), F32))
    if second_at > lines:
        put(lines, jnp.zeros((second_at - lines, LANES), F32))
    early = [p for p in range(len(pieces)) if starts[p] + pieces[p] <= second_at]
    late = [p for p in range(len(pieces)) if p not in early]
    bias = jnp.sum(jnp.sum(gh, axis=0), axis=0, keepdims=True)
    line = iota((C, R), 0)
    blank = jnp.zeros((C, R), F32)
    spare = blank
    for q in range(C // R):
        spare = jnp.where(line == q, bias[:, q * R:(q + 1) * R], spare)
    weight_grad(0, win_in, gs1, spare)
    for p in early:
        reduce_start(p)

    half = (T + 2) // 2 * W
    conv(gs1, w1, pg, 0, half, True)
    reduce_b(0)
    conv(gs1, w1, pg, half, MP - half, True)
    rims = dot(pad_rims, pg[...].astype(BF16)).astype(BF16)
    gact[...] = pg[...].reshape(T + 2, W, C)[1:T + 1]
    ex_start(3, recv_mat, recv_low, rims)
    halo1 = ex_wait(1, recv_mat, recv_low)
    add_halo(pad_act, halo1)
    windows(pad_act, win_act, T + 2)
    weight_grad(second_at, win_act, gs2, blank)
    for p in late:
        reduce_start(p)
    conv(win_act, w2, second, 0, M // 2, False)
    reduce_b(1)
    conv(win_act, w2, second, M // 2, M // 2, False)
    reduce_a(0)
    hi, lo = split(second[...] + pad_in[1:T + 1, 1:W + 1, :].reshape(M, C))
    mean = hot(pool_pos(iota((1, M), 1)) == iota((H * 16, M), 0))
    down = (dot(mean, hi) + dot(mean, lo)) * 0.25
    pooled[...] = down.reshape(H, 16, C)[:, 0:H, :].astype(BF16)
    gather_b(0)
    halo3 = ex_wait(3, send_mat, send_low)
    total = fold(gact, halo3) + gpad2[2:T + 2, 2:T + 2, :]
    gin[...] = total.astype(BF16)
    reduce_a(1)
    gather_b(1)
    gather_face(0)
    gather_face(1)
    gather_end(0)
    gather_end(1)
    for ph in range(4):
        ex_drain(ph)
    for p in range(len(pieces)):
        drain(p)


def finish(C, second_at, pooled_in, gin_in, gath, pooled, gin, gw1, gb1, gw2, wide, bias_row, sem):
    def out(i, src, dst):
        return pltpu.make_async_copy(src, dst, sem.at[i])

    copies = [out(0, pooled_in, pooled), out(1, gin_in, gin)]
    for c in copies:
        c.start()
    half = C - LANES
    for k, (base, dst) in enumerate(((0, gw1), (second_at, gw2))):
        for t in range(9):
            lo = base + t // 2 * 3 * C
            left = gath[lo + t % 2 * C:lo + t % 2 * C + C, :].astype(F32)
            lo = lo + (2 * C if t < 8 else C)
            pair = gath[lo:lo + C, :].astype(F32)
            right = pair[:, 0:half] if t % 2 == 0 else pair[:, half:2 * half]
            wide[k, t // 3, t % 3, :, 0:LANES] = left
            wide[k, t // 3, t % 3, :, LANES:C] = right
            if t % 3 == 2:
                copies.append(out(2 + 3 * k + t // 3, wide.at[k, t // 3], dst.at[t // 3]))
                copies[-1].start()
    bias = gath[13 * C:13 * C + 16, :].astype(F32)
    for q in range(C // half):
        bias_row[:, q * half:(q + 1) * half] = bias[q:q + 1, half:2 * half]
    copies.append(out(8, bias_row, gb1))
    copies[-1].start()
    for c in copies:
        c.wait()


def local(S, F, features, w_first, b_first, w_second, neighbours, rotations, cotangent):
    T, C = features.shape[1], features.shape[2]
    H = T // 2
    D = neighbours.shape[0]
    A = 2 if S % 2 == 0 else 1
    B = S // A
    unit = 16 * F * B
    first = 14 * C // unit
    if first:
        units = (first, -(-28 * C // unit) - first)
    else:
        units = (1, -(-14 * C // unit))
    pieces = tuple(u * unit for u in units)
    rows = sum(pieces)
    K = S + 4 * F
    scale = 1.0 / math.sqrt(D * T * T)
    vm = pl.BlockSpec(memory_space=pltpu.VMEM)
    pooled, gin, gath = pl.pallas_call(
        functools.partial(kernel, S, F, pieces, scale),
        out_shape=(
            pltpu.VMEM((H, H, C), BF16),
            pltpu.VMEM((T, T, C), BF16),
            pltpu.VMEM((rows, LANES), BF16),
        ),
        in_specs=[pl.BlockSpec(memory_space=pl.ANY)] * 7,
        out_specs=(vm,) * 3,
        scratch_shapes=[
            pltpu.SMEM((4, D), jnp.int32),
            pltpu.SMEM((4, D), jnp.int32),
            pltpu.VMEM((T, T, C), BF16),
            pltpu.VMEM((H, H, C), BF16),
            pltpu.VMEM((9 * C, C), BF16),
            pltpu.VMEM((1, C), F32),
            pltpu.VMEM((9 * C, C), BF16),
            pltpu.VMEM((K * W, 4 * W), BF16),
            pltpu.VMEM((K * W, 4 * W), BF16),
            pltpu.VMEM((K * LOW, 8 * W), BF16),
            pltpu.VMEM((K * LOW, 8 * W), BF16),
            pltpu.VMEM((T + 2, W + 8, C), F32),
            pltpu.VMEM((T + 2, W + 8, C), F32),
            pltpu.VMEM((T + 4, W + 8, C), F32),
            pltpu.VMEM((T + 4, W + 8, C), F32),
            pltpu.VMEM((H, 16, C), F32),
            pltpu.VMEM((3, (T + 2) * W, C), BF16),
            pltpu.VMEM((3, (T + 2) * W, C), BF16),
            pltpu.VMEM((3, (T + 4) * W, C), BF16),
            pltpu.VMEM((3, (T + 4) * W, C), BF16),
            pltpu.VMEM((T * W, C), F32),
            pltpu.VMEM((T * W, C), F32),
            pltpu.VMEM(((T + 2) * W, C), F32),
            pltpu.VMEM((T, W, C), F32),
            pltpu.VMEM((4, K, T + LOW, LANES), BF16),
            pltpu.VMEM((4, K, T + LOW, LANES), BF16),
            pltpu.VMEM((rows, LANES), F32),
            pltpu.VMEM((rows, LANES), BF16),
            pltpu.VMEM((F, rows // F, LANES), BF16),
            pltpu.VMEM((rows // F, LANES), BF16),
            pltpu.VMEM((rows // F, LANES), F32),
            pltpu.VMEM((B, rows // (F * B), LANES), BF16),
            pltpu.VMEM((rows // (F * B), LANES), BF16),
            pltpu.VMEM((A, rows // (F * B), LANES), BF16),
            pltpu.SemaphoreType.DMA((4,)),
            pltpu.SemaphoreType.DMA((4,)),
            pltpu.SemaphoreType.DMA((len(pieces), 5)),
            pltpu.SemaphoreType.DMA((len(pieces), 5)),
            pltpu.SemaphoreType.DMA((7,)),
        ],
        compiler_params=pltpu.CompilerParams(
            collective_id=0, has_side_effects=True, vmem_limit_bytes=56 * 1024 * 1024
        ),
        name="level",
    )(
        neighbours.T, rotations.T, features, cotangent,
        w_first.reshape(9 * C, C), b_first.reshape(1, C), w_second.reshape(9 * C, C),
    )
    pooled, gin, gw1, gb1, gw2 = pl.pallas_call(
        functools.partial(finish, C, max(14 * C, pieces[0])),
        out_shape=(
            jax.ShapeDtypeStruct((H, H, C), BF16),
            jax.ShapeDtypeStruct((T, T, C), BF16),
            jax.ShapeDtypeStruct((3, 3, C, C), F32),
            jax.ShapeDtypeStruct((1, C), F32),
            jax.ShapeDtypeStruct((3, 3, C, C), F32),
        ),
        in_specs=[vm] * 3,
        out_specs=(pl.BlockSpec(memory_space=pl.ANY),) * 5,
        scratch_shapes=[
            pltpu.VMEM((2, 3, 3, C, C), F32),
            pltpu.VMEM((1, C), F32),
            pltpu.SemaphoreType.DMA((9,)),
        ],
        compiler_params=pltpu.CompilerParams(vmem_limit_bytes=24 * 1024 * 1024),
        name="finish",
    )(pooled, gin, gath)
    return (pooled, gin, gw1, gb1.reshape(C), gw2)


def solution(mesh):
    tiles = P(("face", "sub"), None, None)
    return jax.shard_map(
        functools.partial(local, mesh.shape["sub"], mesh.shape["face"]),
        mesh=mesh,
        in_specs=(tiles, P(), P(), P(), P(), P(), tiles),
        out_specs=(tiles, tiles, P(), P(), P()),
        check_vma=False,
    )
```

```python
import functools
import math

import jax
import jax.numpy as jnp
from jax import lax
from jax.experimental import pallas as pl
from jax.experimental.pallas import tpu as pltpu
from jax.sharding import PartitionSpec as P

LANES = 128
W = 32
LOW = 16
F32, BF16 = jnp.float32, jnp.bfloat16
MESH = pl.DeviceIdType.MESH


def iota(shape, dim):
    return lax.broadcasted_iota(jnp.int32, shape, dim)


def hot(mask):
    return jnp.where(mask, 1.0, 0.0).astype(BF16)


def dot(a, b, ca=1, cb=0):
    return lax.dot_general(a, b, (((ca,), (cb,)), ((), ())), preferred_element_type=F32)


def split(x):
    hi = x.astype(BF16)
    return hi, (x - hi.astype(F32)).astype(BF16)


def rim_pos(q, extent, pad):
    e, p = q >> 5, (q & (W - 1)) + pad
    far = extent - 1 + 2 * pad
    pos = jnp.where(e == 0, p, jnp.where(e == 1, p * W + far, jnp.where(e == 2, far * W + p, p * W)))
    return jnp.where((q & (W - 1)) < extent, pos, -1)


def pool_pos(r):
    return ((r >> 6) << 4) + ((r & (W - 1)) >> 1)


def kernel(S, F, pieces, scale, nbr_hbm, rot_hbm, feat_hbm, cot_hbm, w1_hbm, b1_hbm, w2_hbm,
           pooled, gin, gath,
           nbr, rot, feat, cot, w1, b1, w2,
           send_mat, recv_mat, send_low, recv_low, pad_in, pad_act, gpad1, gpad2, cotp,
           win_in, win_act, gs1, gs2, hidden, second, pg, gact,
           ex_out, ex_in, wf, wb, w1in, red, accf, w2in, red2, w3in,
           ex_ss, ex_rs, w_ss, w_rs, in_sem):
    T, C = feat.shape[0], feat.shape[2]
    H = T // 2
    face, sub = lax.axis_index("face"), lax.axis_index("sub")
    me = face * S + sub
    A = 2 if S % 2 == 0 else 1
    B = S // A
    a_id, b_id = sub // B, lax.rem(sub, B)
    M, MP = T * W, (T + 2) * W

    def peers(count, mine, body):
        def step(d, c):
            body(lax.rem(mine + d, count))
            return c
        lax.fori_loop(1, count, step, 0)

    def load(i):
        pairs = ((nbr_hbm, nbr), (rot_hbm, rot), (feat_hbm, feat), (w2_hbm, w2), (cot_hbm, cot), (w1_hbm, w1), (b1_hbm, b1))
        return pltpu.make_async_copy(pairs[i][0], pairs[i][1], in_sem.at[i])

    for i in (2, 0, 1, 3, 4, 5, 6):
        load(i).start()

    barrier = pltpu.get_barrier_semaphore()
    peers(S, sub, lambda j: pl.semaphore_signal(barrier, inc=1, device_id=(face, j), device_id_type=MESH))
    peers(F, face, lambda f: pl.semaphore_signal(barrier, inc=1, device_id=(f, sub), device_id_type=MESH))

    p32 = iota((W, 4 * W), 0)
    c32 = iota((W, 4 * W), 1)

    q16 = iota((LOW, 8 * W), 0)
    d16 = iota((LOW, 8 * W), 1)
    low_pix = q16 + jnp.where(d16 >= 4 * W, H, 0)
    low_col = d16 & (4 * W - 1)

    def put_send(k, hit, src, flip):
        tgt = jnp.where(flip == 1, src * W + T - 1 - p32, src * W + p32)
        send_mat[pl.ds(pl.multiple_of(k * W, W), W), :] = hot((c32 == tgt) & (p32 < T) & (hit == 1))
        tgt = jnp.where(flip == 1, src * W + T - 1 - low_pix, src * W + low_pix)
        send_low[pl.ds(pl.multiple_of(k * LOW, LOW), LOW), :] = hot((low_col == tgt) & (q16 < H) & (hit == 1))

    def put_recv(k, edge):
        recv_mat[pl.ds(pl.multiple_of(k * W, W), W), :] = hot((c32 == edge * W + p32) & (p32 < T) & (edge >= 0))
        recv_low[pl.ds(pl.multiple_of(k * LOW, LOW), LOW), :] = hot(
            (low_col == edge * W + low_pix) & (q16 < H) & (edge >= 0))

    def edge_code(tile, e):
        r = rot[e, tile]
        x = (e + 2) % 4
        src = (x + r) & 3
        odd = x % 2
        flip = jnp.where(r == 2, 1, jnp.where(r == 1, odd, jnp.where(r == 3, 1 - odd, 0)))
        return nbr[e, tile] == me, src, flip

    def send_in_face(j, c):
        hit, src, flip = jnp.int32(0), jnp.int32(0), jnp.int32(0)
        for e in range(4):
            h, s, f = edge_code(face * S + j, e)
            hit = jnp.where(h, 1, hit)
            src = jnp.where(h, s, src)
            flip = jnp.where(h, f, flip)
        put_send(j, hit, src, flip)
        return c

    def send_cross(f, c):
        for e in range(4):
            h, s, fl = edge_code(f * S + sub, e)
            put_send(S + f * 4 + e, jnp.where(h & (f != face), 1, 0), s, fl)
        return c

    def recv_in_face(j, c):
        edge = jnp.int32(-1)
        for e in range(4):
            edge = jnp.where(nbr[e, me] == face * S + j, e, edge)
        put_recv(j, edge)
        return c

    def recv_cross(f, c):
        for e in range(4):
            put_recv(S + f * 4 + e, jnp.where((nbr[e, me] == f * S + sub) & (f != face), e, -1))
        return c

    def ex_sub(ph, j, s_in):
        return pltpu.make_async_remote_copy(
            src_ref=ex_out.at[ph, j], dst_ref=ex_in.at[ph, s_in],
            send_sem=ex_ss.at[ph], recv_sem=ex_rs.at[ph],
            device_id=(face, j), device_id_type=MESH)

    def ex_face(ph, f, f_in):
        return pltpu.make_async_remote_copy(
            src_ref=ex_out.at[ph, pl.ds(S + 4 * f, 4)], dst_ref=ex_in.at[ph, pl.ds(S + 4 * f_in, 4)],
            send_sem=ex_ss.at[ph], recv_sem=ex_rs.at[ph],
            device_id=(f, sub), device_id_type=MESH)

    slots = S + 4 * F
    R = C - LANES

    def ex_start(ph, mat, low, rims):
        zero = jnp.zeros((4 * W, R), BF16)
        wide = jnp.concatenate([
            jnp.concatenate([rims[:, LANES:C], zero], axis=1),
            jnp.concatenate([zero, rims[:, LANES:C]], axis=1)], axis=0)
        top = dot(mat[...], rims[:, 0:LANES]).reshape(slots, W, LANES)[:, 0:T, :]
        bottom = dot(low[...], wide).reshape(slots, LOW, LANES)
        ex_out[ph] = jnp.concatenate([top, bottom], axis=1).astype(BF16)
        peers(F, face, lambda f: ex_face(ph, f, face).start())
        def step(d, c):
            ex_sub(ph, lax.rem(sub + S - d, S), sub).start()
            return c
        lax.fori_loop(1, S, step, 0)

    def take(ref, sem):
        pltpu.make_async_copy(ref, ref, sem).wait()

    ex_count = S - 1 + (F - 1) * 4

    def ex_wait(ph, mat, low):
        take(ex_in.at[ph, 0:ex_count], ex_rs.at[ph])
        got = ex_in[ph].astype(F32)
        left = dot(mat[...], got[:, 0:W, :].reshape(slots * W, LANES).astype(BF16), 0, 0)
        rest = dot(low[...], got[:, T:T + LOW, :].reshape(slots * LOW, LANES).astype(BF16), 0, 0)
        rest = rest[0:4 * W, 0:R] + rest[4 * W:8 * W, R:2 * R]
        return jnp.concatenate([left, rest], axis=1)

    def ex_drain(ph):
        take(ex_out.at[ph, 0:ex_count], ex_ss.at[ph])


    def windows(src, dst, rows):
        for b in range(3):
            dst[b] = src[:, b:b + W, :].reshape(rows * W, C).astype(BF16)

    def add_halo(padded, halo):
        pad_place = hot(iota((MP, 4 * W), 0) == rim_pos(iota((1, 4 * W), 1), T, 1))
        placed = dot(pad_place, halo.astype(BF16)).reshape(T + 2, W, C)
        padded[:, 0:W, :] = padded[:, 0:W, :] + placed

    def conv(win, wt, out, lo, n, back):
        acc = None
        for a in range(3):
            for b in range(3):
                x = win[b, lo + a * W:lo + a * W + n, :]
                tap = (2 - a) * 3 + 2 - b if back else a * 3 + b
                d = dot(x, wt[tap * C:(tap + 1) * C, :], 1, 1 if back else 0)
                acc = d if acc is None else acc + d
        out[lo:lo + n, :] = acc

    def put(r, v):
        wf[r:r + v.shape[0], :] = v
        wb[r:r + v.shape[0], :] = v.astype(BF16)

    def weight_grad(base, win, gs, spare):
        for t in range(9):
            a, b = t // 3, t % 3
            v = dot(win[b], gs[2, (2 - a) * W:(2 - a) * W + MP, :], 0, 0)
            at = base + t // 2 * 3 * C
            put(at + t % 2 * C, v[:, 0:LANES])
            rest = v[:, LANES:C]
            if t % 2 == 0:
                even = rest
            if t % 2 == 1:
                put(at + 2 * C, jnp.concatenate([even, rest], axis=1))
            if t == 8:
                put(at + C, jnp.concatenate([rest, spare], axis=1))

    pad_in[...] = jnp.zeros(pad_in.shape, F32)
    load(0).wait()
    load(1).wait()
    lax.fori_loop(0, S, send_in_face, 0)
    lax.fori_loop(0, F, send_cross, 0)
    own_rims = hot(iota((4 * W, M), 1) == rim_pos(iota((4 * W, 1), 0), T, 0))
    load(2).wait()
    pad_in[1:T + 1, 1:T + 1, :] = feat[...].astype(F32)
    flat_in = pad_in[1:T + 1, 1:W + 1, :].reshape(M, C)
    rims = dot(own_rims, flat_in.astype(BF16)).astype(BF16)
    pl.semaphore_wait(barrier, S + F - 2)
    ex_start(0, send_mat, send_low, rims)

    lax.fori_loop(0, S, recv_in_face, 0)
    lax.fori_loop(0, F, recv_cross, 0)
    cotp[...] = jnp.zeros(cotp.shape, F32)
    load(4).wait()
    cotp[:, 0:H, :] = cot[...].astype(F32)
    spread = hot(pool_pos(iota((M, 1), 0)) == iota((M, H * 16), 1))
    up = dot(spread, cotp[...].reshape(H * 16, C).astype(BF16)) * 0.25
    gpad2[...] = jnp.zeros(gpad2.shape, F32)
    gpad2[2:T + 2, 2:T + 2, :] = up.reshape(T, W, C)[:, 0:T, :]
    windows(gpad2, gs2, T + 4)
    load(3).wait()
    conv(gs2, w2, pg, 0, MP, True)
    pad_rims = hot(iota((4 * W, MP), 1) == rim_pos(iota((4 * W, 1), 0), T, 1))
    rims = dot(pad_rims, pg[...].astype(BF16)).astype(BF16)
    ex_start(2, recv_mat, recv_low, rims)
    gact[...] = pg[...].reshape(T + 2, W, C)[1:T + 1]
    pad_act[...] = jnp.zeros(pad_act.shape, F32)
    gpad1[...] = jnp.zeros(gpad1.shape, F32)
    for ph in range(4):
        ex_in[ph, sub] = jnp.zeros((T + LOW, LANES), BF16)
        ex_in[ph, pl.ds(S + 4 * face, 4)] = jnp.zeros((4, T + LOW, LANES), BF16)

    halo0 = ex_wait(0, recv_mat, recv_low)
    add_halo(pad_in, halo0)
    windows(pad_in, win_in, T + 2)
    load(5).wait()
    load(6).wait()
    conv(win_in, w1, hidden, 0, M, False)
    hid = hidden[...] + b1[...]
    sig = 1.0 / (1.0 + jnp.exp(-hid))
    act = (hid * sig).astype(BF16)
    rims = dot(own_rims, act).astype(BF16)
    ex_start(1, send_mat, send_low, rims)
    pad_act[1:T + 1, 1:T + 1, :] = act.astype(F32).reshape(T, W, C)[:, 0:T, :]
    slope = (sig * (1.0 + hid * (1.0 - sig))).reshape(T, W, C)[:, 0:T, :]

    def fold(middle, arrived):
        own_place = hot(iota((M, 4 * W), 0) == rim_pos(iota((1, 4 * W), 1), T, 0))
        hi, lo = split(arrived)
        back = dot(own_place, hi) + dot(own_place, lo)
        return middle[:, 1:T + 1, :] + back.reshape(T, W, C)[:, 0:T, :]

    halo2 = ex_wait(2, send_mat, send_low)
    ga = fold(gact, halo2).astype(BF16).astype(F32)
    gh = (ga * slope).astype(BF16).astype(F32)
    gpad1[2:T + 2, 2:T + 2, :] = gh
    windows(gpad1, gs1, T + 4)

    D = S * F
    starts = [sum(pieces[:p]) for p in range(len(pieces))]

    def whole(p, level):
        share = F if level == 0 else F * B
        return slice(starts[p] // share, (starts[p] + pieces[p]) // share)

    def spot(ref, p, start, size):
        return ref.at[pl.ds(pl.multiple_of(starts[p] + start, 16), size), :]

    def sizes(p):
        return pieces[p] // F, pieces[p] // (F * B)

    def remote(p, st, src, dst, device):
        return pltpu.make_async_remote_copy(
            src_ref=src, dst_ref=dst, send_sem=w_ss.at[p, st], recv_sem=w_rs.at[p, st],
            device_id=device, device_id_type=MESH)

    def to_face(f):
        return (f, sub)

    def to_b(j):
        return (face, a_id * B + j)

    def to_a(j):
        return (face, j * B + b_id)

    def face_copy(p, f, f_in):
        part = sizes(p)[0]
        return remote(p, 0, spot(wb, p, f * part, part), w1in.at[f_in, whole(p, 0)], to_face(f))

    def b_copy(p, j, j_in):
        group = sizes(p)[1]
        at = pl.ds(pl.multiple_of(starts[p] // F + j * group, 16), group)
        return remote(p, 1, red.at[at, :], w2in.at[j_in, whole(p, 1)], to_b(j))

    def a_copy(p, j, j_in):
        return remote(p, 2, red2.at[whole(p, 1)], w3in.at[j_in, whole(p, 1)], to_a(j))

    def b_gather(p, j, own):
        part, group = sizes(p)
        place = spot(gath, p, face * part + own * group, group)
        return remote(p, 3, place, place, to_b(j))

    def face_gather(p, f, own):
        part = sizes(p)[0]
        place = spot(gath, p, own * part, part)
        return remote(p, 4, place, place, to_face(f))

    counts = (F - 1, B - 1, A - 1, B - 1, F - 1)

    def moved(p, st):
        return counts[st] * sizes(p)[(0, 1, 1, 1, 0)[st]]

    def arrived_all(p, st):
        if counts[st]:
            if st < 3:
                take((w1in, w2in, w3in)[st].at[0:counts[st], whole(p, st)], w_rs.at[p, st])
            else:
                take(gath.at[starts[p]:starts[p] + moved(p, st), :], w_rs.at[p, st])

    def reduce_start(p):
        peers(F, face, lambda f: face_copy(p, f, face).start())

    def summed(first, count, mine, ref, span):
        def step(d, tot):
            return tot + ref[lax.rem(mine + d, count), span, :].astype(F32)
        return lax.fori_loop(1, count, step, first)

    def reduce_b(p):
        arrived_all(p, 0)
        part, group = sizes(p)
        lo = starts[p] // F
        for r in range(B):
            tot = wf[pl.ds(pl.multiple_of(starts[p] + face * part + r * group, 16), group), :]
            for f in range(1, F):
                tot = tot + w1in[lax.rem(face + f, F), lo + r * group:lo + (r + 1) * group, :].astype(F32)
            accf[lo + r * group:lo + (r + 1) * group, :] = tot
            red[lo + r * group:lo + (r + 1) * group, :] = tot.astype(BF16)
        peers(B, b_id, lambda j: b_copy(p, j, b_id).start())

    def reduce_a(p):
        arrived_all(p, 1)
        group = sizes(p)[1]
        own = pl.ds(pl.multiple_of(starts[p] // F + b_id * group, 16), group)
        tot = summed(accf[own, :], B, b_id, w2in, whole(p, 1))
        red2[whole(p, 1), :] = tot.astype(BF16)
        peers(A, a_id, lambda j: a_copy(p, j, a_id).start())

    def gather_b(p):
        arrived_all(p, 2)
        part, group = sizes(p)
        tot = summed(red2[whole(p, 1), :].astype(F32), A, a_id, w3in, whole(p, 1))
        own = pl.ds(pl.multiple_of(starts[p] + face * part + b_id * group, 16), group)
        gath[own, :] = (tot * scale).astype(BF16)
        peers(B, b_id, lambda j: b_gather(p, j, b_id).start())

    def gather_face(p):
        arrived_all(p, 3)
        peers(F, face, lambda f: face_gather(p, f, face).start())

    def gather_end(p):
        arrived_all(p, 4)

    def drain(p):
        for st in range(5):
            if counts[st]:
                lo = starts[p] // (1, F, F * B, 1, 1)[st]
                take((wb, red, red2, gath, gath)[st].at[lo:lo + moved(p, st), :], w_ss.at[p, st])

    lines = 14 * C
    second_at = max(lines, starts[1])
    used = second_at + lines
    if wf.shape[0] > used:
        put(used, jnp.zeros((wf.shape[0] - used, LANES), F32))
    if second_at > lines:
        put(lines, jnp.zeros((second_at - lines, LANES), F32))
    early = [p for p in range(len(pieces)) if starts[p] + pieces[p] <= second_at]
    late = [p for p in range(len(pieces)) if p not in early]
    bias = jnp.sum(jnp.sum(gh, axis=0), axis=0, keepdims=True)
    line = iota((C, R), 0)
    blank = jnp.zeros((C, R), F32)
    spare = blank
    for q in range(C // R):
        spare = jnp.where(line == q, bias[:, q * R:(q + 1) * R], spare)
    weight_grad(0, win_in, gs1, spare)
    for p in early:
        reduce_start(p)

    half = (T + 2) // 2 * W
    conv(gs1, w1, pg, 0, half, True)
    reduce_b(0)
    halo1 = ex_wait(1, recv_mat, recv_low)
    add_halo(pad_act, halo1)
    windows(pad_act, win_act, T + 2)
    weight_grad(second_at, win_act, gs2, blank)
    for p in late:
        reduce_start(p)
    conv(win_act, w2, second, 0, M // 2, False)
    reduce_b(1)
    conv(gs1, w1, pg, half, MP - half, True)
    rims = dot(pad_rims, pg[...].astype(BF16)).astype(BF16)
    gact[...] = pg[...].reshape(T + 2, W, C)[1:T + 1]
    reduce_a(0)
    ex_start(3, recv_mat, recv_low, rims)
    conv(win_act, w2, second, M // 2, M // 2, False)
    hi, lo = split(second[...] + pad_in[1:T + 1, 1:W + 1, :].reshape(M, C))
    mean = hot(pool_pos(iota((1, M), 1)) == iota((H * 16, M), 0))
    down = (dot(mean, hi) + dot(mean, lo)) * 0.25
    pooled[...] = down.reshape(H, 16, C)[:, 0:H, :].astype(BF16)
    reduce_a(1)
    gather_b(0)
    gather_b(1)
    halo3 = ex_wait(3, send_mat, send_low)
    total = fold(gact, halo3) + gpad2[2:T + 2, 2:T + 2, :]
    gin[...] = total.astype(BF16)
    gather_face(0)
    gather_face(1)
    gather_end(0)
    gather_end(1)
    for ph in range(4):
        ex_drain(ph)
    for p in range(len(pieces)):
        drain(p)


def finish(C, second_at, pooled_in, gin_in, gath, pooled, gin, gw1, gb1, gw2, wide, bias_row, sem):
    def out(i, src, dst):
        return pltpu.make_async_copy(src, dst, sem.at[i])

    copies = [out(0, pooled_in, pooled), out(1, gin_in, gin)]
    for c in copies:
        c.start()
    half = C - LANES
    for k, (base, dst) in enumerate(((0, gw1), (second_at, gw2))):
        for t in range(9):
            lo = base + t // 2 * 3 * C
            left = gath[lo + t % 2 * C:lo + t % 2 * C + C, :].astype(F32)
            lo = lo + (2 * C if t < 8 else C)
            pair = gath[lo:lo + C, :].astype(F32)
            right = pair[:, 0:half] if t % 2 == 0 else pair[:, half:2 * half]
            wide[k, t // 3, t % 3, :, 0:LANES] = left
            wide[k, t // 3, t % 3, :, LANES:C] = right
            if t % 3 == 2:
                copies.append(out(2 + 3 * k + t // 3, wide.at[k, t // 3], dst.at[t // 3]))
                copies[-1].start()
    bias = gath[13 * C:13 * C + 16, :].astype(F32)
    for q in range(C // half):
        bias_row[:, q * half:(q + 1) * half] = bias[q:q + 1, half:2 * half]
    copies.append(out(8, bias_row, gb1))
    copies[-1].start()
    for c in copies:
        c.wait()


def local(S, F, features, w_first, b_first, w_second, neighbours, rotations, cotangent):
    T, C = features.shape[1], features.shape[2]
    H = T // 2
    D = neighbours.shape[0]
    A = 2 if S % 2 == 0 else 1
    B = S // A
    unit = 16 * F * B
    first = 14 * C // unit
    if first:
        units = (first, -(-28 * C // unit) - first)
    else:
        units = (1, -(-14 * C // unit))
    pieces = tuple(u * unit for u in units)
    rows = sum(pieces)
    K = S + 4 * F
    scale = 1.0 / math.sqrt(D * T * T)
    vm = pl.BlockSpec(memory_space=pltpu.VMEM)
    pooled, gin, gath = pl.pallas_call(
        functools.partial(kernel, S, F, pieces, scale),
        out_shape=(
            pltpu.VMEM((H, H, C), BF16),
            pltpu.VMEM((T, T, C), BF16),
            pltpu.VMEM((rows, LANES), BF16),
        ),
        in_specs=[pl.BlockSpec(memory_space=pl.ANY)] * 7,
        out_specs=(vm,) * 3,
        scratch_shapes=[
            pltpu.SMEM((4, D), jnp.int32),
            pltpu.SMEM((4, D), jnp.int32),
            pltpu.VMEM((T, T, C), BF16),
            pltpu.VMEM((H, H, C), BF16),
            pltpu.VMEM((9 * C, C), BF16),
            pltpu.VMEM((1, C), F32),
            pltpu.VMEM((9 * C, C), BF16),
            pltpu.VMEM((K * W, 4 * W), BF16),
            pltpu.VMEM((K * W, 4 * W), BF16),
            pltpu.VMEM((K * LOW, 8 * W), BF16),
            pltpu.VMEM((K * LOW, 8 * W), BF16),
            pltpu.VMEM((T + 2, W + 8, C), F32),
            pltpu.VMEM((T + 2, W + 8, C), F32),
            pltpu.VMEM((T + 4, W + 8, C), F32),
            pltpu.VMEM((T + 4, W + 8, C), F32),
            pltpu.VMEM((H, 16, C), F32),
            pltpu.VMEM((3, (T + 2) * W, C), BF16),
            pltpu.VMEM((3, (T + 2) * W, C), BF16),
            pltpu.VMEM((3, (T + 4) * W, C), BF16),
            pltpu.VMEM((3, (T + 4) * W, C), BF16),
            pltpu.VMEM((T * W, C), F32),
            pltpu.VMEM((T * W, C), F32),
            pltpu.VMEM(((T + 2) * W, C), F32),
            pltpu.VMEM((T, W, C), F32),
            pltpu.VMEM((4, K, T + LOW, LANES), BF16),
            pltpu.VMEM((4, K, T + LOW, LANES), BF16),
            pltpu.VMEM((rows, LANES), F32),
            pltpu.VMEM((rows, LANES), BF16),
            pltpu.VMEM((F, rows // F, LANES), BF16),
            pltpu.VMEM((rows // F, LANES), BF16),
            pltpu.VMEM((rows // F, LANES), F32),
            pltpu.VMEM((B, rows // (F * B), LANES), BF16),
            pltpu.VMEM((rows // (F * B), LANES), BF16),
            pltpu.VMEM((A, rows // (F * B), LANES), BF16),
            pltpu.SemaphoreType.DMA((4,)),
            pltpu.SemaphoreType.DMA((4,)),
            pltpu.SemaphoreType.DMA((len(pieces), 5)),
            pltpu.SemaphoreType.DMA((len(pieces), 5)),
            pltpu.SemaphoreType.DMA((7,)),
        ],
        compiler_params=pltpu.CompilerParams(
            collective_id=0, has_side_effects=True, vmem_limit_bytes=56 * 1024 * 1024
        ),
        name="level",
    )(
        neighbours.T, rotations.T, features, cotangent,
        w_first.reshape(9 * C, C), b_first.reshape(1, C), w_second.reshape(9 * C, C),
    )
    pooled, gin, gw1, gb1, gw2 = pl.pallas_call(
        functools.partial(finish, C, max(14 * C, pieces[0])),
        out_shape=(
            jax.ShapeDtypeStruct((H, H, C), BF16),
            jax.ShapeDtypeStruct((T, T, C), BF16),
            jax.ShapeDtypeStruct((3, 3, C, C), F32),
            jax.ShapeDtypeStruct((1, C), F32),
            jax.ShapeDtypeStruct((3, 3, C, C), F32),
        ),
        in_specs=[vm] * 3,
        out_specs=(pl.BlockSpec(memory_space=pl.ANY),) * 5,
        scratch_shapes=[
            pltpu.VMEM((2, 3, 3, C, C), F32),
            pltpu.VMEM((1, C), F32),
            pltpu.SemaphoreType.DMA((9,)),
        ],
        compiler_params=pltpu.CompilerParams(vmem_limit_bytes=24 * 1024 * 1024),
        name="finish",
    )(pooled, gin, gath)
    return (pooled, gin, gw1, gb1.reshape(C), gw2)


def solution(mesh):
    tiles = P(("face", "sub"), None, None)
    return jax.shard_map(
        functools.partial(local, mesh.shape["sub"], mesh.shape["face"]),
        mesh=mesh,
        in_specs=(tiles, P(), P(), P(), P(), P(), tiles),
        out_specs=(tiles, tiles, P(), P(), P()),
        check_vma=False,
    )
```

```python
import functools
import math

import jax
import jax.numpy as jnp
from jax import lax
from jax.experimental import pallas as pl
from jax.experimental.pallas import tpu as pltpu
from jax.sharding import PartitionSpec as P

LANES = 128
W = 32
LOW = 16
F32, BF16 = jnp.float32, jnp.bfloat16
MESH = pl.DeviceIdType.MESH


def iota(shape, dim):
    return lax.broadcasted_iota(jnp.int32, shape, dim)


def hot(mask):
    return jnp.where(mask, 1.0, 0.0).astype(BF16)


def dot(a, b, ca=1, cb=0):
    return lax.dot_general(a, b, (((ca,), (cb,)), ((), ())), preferred_element_type=F32)


def split(x):
    hi = x.astype(BF16)
    return hi, (x - hi.astype(F32)).astype(BF16)


def rim_pos(q, extent, pad):
    e, p = q >> 5, (q & (W - 1)) + pad
    far = extent - 1 + 2 * pad
    pos = jnp.where(e == 0, p, jnp.where(e == 1, p * W + far, jnp.where(e == 2, far * W + p, p * W)))
    return jnp.where((q & (W - 1)) < extent, pos, -1)


def pool_pos(r):
    return ((r >> 6) << 4) + ((r & (W - 1)) >> 1)


def kernel(S, F, pieces, scale, nbr_hbm, rot_hbm, feat_hbm, cot_hbm, w1_hbm, b1_hbm, w2_hbm,
           pooled, gin, gath,
           nbr, rot, feat, cot, w1, b1, w2,
           send_mat, recv_mat, send_low, recv_low, pad_in, pad_act, gpad1, gpad2, cotp,
           win_in, win_act, gs1, gs2, hidden, second, pg, gact,
           ex_out, ex_in, wf, wb, w1in, red, accf, w2in, red2, w3in,
           ex_ss, ex_rs, w_ss, w_rs, in_sem):
    T, C = feat.shape[0], feat.shape[2]
    H = T // 2
    face, sub = lax.axis_index("face"), lax.axis_index("sub")
    me = face * S + sub
    A = 2 if S % 2 == 0 else 1
    B = S // A
    a_id, b_id = sub // B, lax.rem(sub, B)
    M, MP = T * W, (T + 2) * W

    def peers(count, mine, body):
        def step(d, c):
            body(lax.rem(mine + d, count))
            return c
        lax.fori_loop(1, count, step, 0)

    def load(i):
        pairs = ((nbr_hbm, nbr), (rot_hbm, rot), (feat_hbm, feat), (w2_hbm, w2), (cot_hbm, cot), (w1_hbm, w1), (b1_hbm, b1))
        return pltpu.make_async_copy(pairs[i][0], pairs[i][1], in_sem.at[i])

    for i in (2, 0, 1, 3, 4, 5, 6):
        load(i).start()

    barrier = pltpu.get_barrier_semaphore()
    peers(S, sub, lambda j: pl.semaphore_signal(barrier, inc=1, device_id=(face, j), device_id_type=MESH))
    peers(F, face, lambda f: pl.semaphore_signal(barrier, inc=1, device_id=(f, sub), device_id_type=MESH))

    p32 = iota((W, 4 * W), 0)
    c32 = iota((W, 4 * W), 1)

    q16 = iota((LOW, 8 * W), 0)
    d16 = iota((LOW, 8 * W), 1)
    low_pix = q16 + jnp.where(d16 >= 4 * W, H, 0)
    low_col = d16 & (4 * W - 1)

    def put_send(k, hit, src, flip):
        tgt = jnp.where(flip == 1, src * W + T - 1 - p32, src * W + p32)
        send_mat[pl.ds(pl.multiple_of(k * W, W), W), :] = hot((c32 == tgt) & (p32 < T) & (hit == 1))
        tgt = jnp.where(flip == 1, src * W + T - 1 - low_pix, src * W + low_pix)
        send_low[pl.ds(pl.multiple_of(k * LOW, LOW), LOW), :] = hot((low_col == tgt) & (q16 < H) & (hit == 1))

    def put_recv(k, edge):
        recv_mat[pl.ds(pl.multiple_of(k * W, W), W), :] = hot((c32 == edge * W + p32) & (p32 < T) & (edge >= 0))
        recv_low[pl.ds(pl.multiple_of(k * LOW, LOW), LOW), :] = hot(
            (low_col == edge * W + low_pix) & (q16 < H) & (edge >= 0))

    def edge_code(tile, e):
        r = rot[e, tile]
        x = (e + 2) % 4
        src = (x + r) & 3
        odd = x % 2
        flip = jnp.where(r == 2, 1, jnp.where(r == 1, odd, jnp.where(r == 3, 1 - odd, 0)))
        return nbr[e, tile] == me, src, flip

    def send_in_face(j, c):
        hit, src, flip = jnp.int32(0), jnp.int32(0), jnp.int32(0)
        for e in range(4):
            h, s, f = edge_code(face * S + j, e)
            hit = jnp.where(h, 1, hit)
            src = jnp.where(h, s, src)
            flip = jnp.where(h, f, flip)
        put_send(j, hit, src, flip)
        return c

    def send_cross(f, c):
        for e in range(4):
            h, s, fl = edge_code(f * S + sub, e)
            put_send(S + f * 4 + e, jnp.where(h & (f != face), 1, 0), s, fl)
        return c

    def recv_in_face(j, c):
        edge = jnp.int32(-1)
        for e in range(4):
            edge = jnp.where(nbr[e, me] == face * S + j, e, edge)
        put_recv(j, edge)
        return c

    def recv_cross(f, c):
        for e in range(4):
            put_recv(S + f * 4 + e, jnp.where((nbr[e, me] == f * S + sub) & (f != face), e, -1))
        return c

    def ex_sub(ph, j, s_in):
        return pltpu.make_async_remote_copy(
            src_ref=ex_out.at[ph, j], dst_ref=ex_in.at[ph, s_in],
            send_sem=ex_ss.at[0], recv_sem=ex_rs.at[ph],
            device_id=(face, j), device_id_type=MESH)

    def ex_face(ph, f, f_in):
        return pltpu.make_async_remote_copy(
            src_ref=ex_out.at[ph, pl.ds(S + 4 * f, 4)], dst_ref=ex_in.at[ph, pl.ds(S + 4 * f_in, 4)],
            send_sem=ex_ss.at[0], recv_sem=ex_rs.at[ph],
            device_id=(f, sub), device_id_type=MESH)

    slots = S + 4 * F
    R = C - LANES

    def ex_start(ph, mat, low, rims):
        zero = jnp.zeros((4 * W, R), BF16)
        wide = jnp.concatenate([
            jnp.concatenate([rims[:, LANES:C], zero], axis=1),
            jnp.concatenate([zero, rims[:, LANES:C]], axis=1)], axis=0)
        top = dot(mat[...], rims[:, 0:LANES]).reshape(slots, W, LANES)[:, 0:T, :]
        bottom = dot(low[...], wide).reshape(slots, LOW, LANES)
        ex_out[ph] = jnp.concatenate([top, bottom], axis=1).astype(BF16)
        peers(F, face, lambda f: ex_face(ph, f, face).start())
        def step(d, c):
            ex_sub(ph, lax.rem(sub + S - d, S), sub).start()
            return c
        lax.fori_loop(1, S, step, 0)

    def take(ref, sem):
        pltpu.make_async_copy(ref, ref, sem).wait()

    ex_count = S - 1 + (F - 1) * 4

    def ex_wait(ph, mat, low):
        take(ex_in.at[ph, 0:ex_count], ex_rs.at[ph])
        got = ex_in[ph].astype(F32)
        left = dot(mat[...], got[:, 0:W, :].reshape(slots * W, LANES).astype(BF16), 0, 0)
        rest = dot(low[...], got[:, T:T + LOW, :].reshape(slots * LOW, LANES).astype(BF16), 0, 0)
        rest = rest[0:4 * W, 0:R] + rest[4 * W:8 * W, R:2 * R]
        return jnp.concatenate([left, rest], axis=1)

    def ex_drain():
        take(ex_out.at[:, 0:ex_count], ex_ss.at[0])


    def windows(src, dst, rows):
        for b in range(3):
            dst[b] = src[:, b:b + W, :].reshape(rows * W, C).astype(BF16)

    def add_halo(padded, halo):
        pad_place = hot(iota((MP, 4 * W), 0) == rim_pos(iota((1, 4 * W), 1), T, 1))
        placed = dot(pad_place, halo.astype(BF16)).reshape(T + 2, W, C)
        padded[:, 0:W, :] = padded[:, 0:W, :] + placed

    def conv(win, wt, out, lo, n, back):
        acc = None
        for a in range(3):
            for b in range(3):
                x = win[b, lo + a * W:lo + a * W + n, :]
                tap = (2 - a) * 3 + 2 - b if back else a * 3 + b
                d = dot(x, wt[tap * C:(tap + 1) * C, :], 1, 1 if back else 0)
                acc = d if acc is None else acc + d
        out[lo:lo + n, :] = acc

    def put(r, v):
        wf[r:r + v.shape[0], :] = v
        wb[r:r + v.shape[0], :] = v.astype(BF16)

    def weight_grad(base, win, gs, spare):
        for t in range(9):
            a, b = t // 3, t % 3
            v = dot(win[b], gs[2, (2 - a) * W:(2 - a) * W + MP, :], 0, 0)
            at = base + t // 2 * 3 * C
            put(at + t % 2 * C, v[:, 0:LANES])
            rest = v[:, LANES:C]
            if t % 2 == 0:
                even = rest
            if t % 2 == 1:
                put(at + 2 * C, jnp.concatenate([even, rest], axis=1))
            if t == 8:
                put(at + C, jnp.concatenate([rest, spare], axis=1))

    pad_in[...] = jnp.zeros(pad_in.shape, F32)
    load(0).wait()
    load(1).wait()
    lax.fori_loop(0, S, send_in_face, 0)
    lax.fori_loop(0, F, send_cross, 0)
    own_rims = hot(iota((4 * W, M), 1) == rim_pos(iota((4 * W, 1), 0), T, 0))
    load(2).wait()
    pad_in[1:T + 1, 1:T + 1, :] = feat[...].astype(F32)
    flat_in = pad_in[1:T + 1, 1:W + 1, :].reshape(M, C)
    rims = dot(own_rims, flat_in.astype(BF16)).astype(BF16)
    pl.semaphore_wait(barrier, S + F - 2)
    ex_start(0, send_mat, send_low, rims)

    lax.fori_loop(0, S, recv_in_face, 0)
    lax.fori_loop(0, F, recv_cross, 0)
    cotp[...] = jnp.zeros(cotp.shape, F32)
    load(4).wait()
    cotp[:, 0:H, :] = cot[...].astype(F32)
    spread = hot(pool_pos(iota((M, 1), 0)) == iota((M, H * 16), 1))
    up = dot(spread, cotp[...].reshape(H * 16, C).astype(BF16)) * 0.25
    gpad2[...] = jnp.zeros(gpad2.shape, F32)
    gpad2[2:T + 2, 2:T + 2, :] = up.reshape(T, W, C)[:, 0:T, :]
    windows(gpad2, gs2, T + 4)
    load(3).wait()
    conv(gs2, w2, pg, 0, MP, True)
    pad_rims = hot(iota((4 * W, MP), 1) == rim_pos(iota((4 * W, 1), 0), T, 1))
    rims = dot(pad_rims, pg[...].astype(BF16)).astype(BF16)
    ex_start(2, recv_mat, recv_low, rims)
    gact[...] = pg[...].reshape(T + 2, W, C)[1:T + 1]
    pad_act[...] = jnp.zeros(pad_act.shape, F32)
    gpad1[...] = jnp.zeros(gpad1.shape, F32)
    for ph in range(4):
        ex_in[ph, sub] = jnp.zeros((T + LOW, LANES), BF16)
        ex_in[ph, pl.ds(S + 4 * face, 4)] = jnp.zeros((4, T + LOW, LANES), BF16)

    halo0 = ex_wait(0, recv_mat, recv_low)
    add_halo(pad_in, halo0)
    windows(pad_in, win_in, T + 2)
    load(5).wait()
    load(6).wait()
    conv(win_in, w1, hidden, 0, M, False)
    hid = hidden[...] + b1[...]
    sig = 1.0 / (1.0 + jnp.exp(-hid))
    act = (hid * sig).astype(BF16)
    rims = dot(own_rims, act).astype(BF16)
    ex_start(1, send_mat, send_low, rims)
    pad_act[1:T + 1, 1:T + 1, :] = act.astype(F32).reshape(T, W, C)[:, 0:T, :]
    slope = (sig * (1.0 + hid * (1.0 - sig))).reshape(T, W, C)[:, 0:T, :]

    def fold(middle, arrived):
        own_place = hot(iota((M, 4 * W), 0) == rim_pos(iota((1, 4 * W), 1), T, 0))
        hi, lo = split(arrived)
        back = dot(own_place, hi) + dot(own_place, lo)
        return middle[:, 1:T + 1, :] + back.reshape(T, W, C)[:, 0:T, :]

    halo2 = ex_wait(2, send_mat, send_low)
    ga = fold(gact, halo2).astype(BF16).astype(F32)
    gh = (ga * slope).astype(BF16).astype(F32)
    gpad1[2:T + 2, 2:T + 2, :] = gh
    windows(gpad1, gs1, T + 4)

    D = S * F
    starts = [sum(pieces[:p]) for p in range(len(pieces))]

    def whole(p, level):
        share = F if level == 0 else F * B
        return slice(starts[p] // share, (starts[p] + pieces[p]) // share)

    def spot(ref, p, start, size):
        return ref.at[pl.ds(pl.multiple_of(starts[p] + start, 16), size), :]

    def sizes(p):
        return pieces[p] // F, pieces[p] // (F * B)

    def remote(p, st, src, dst, device):
        return pltpu.make_async_remote_copy(
            src_ref=src, dst_ref=dst, send_sem=w_ss.at[0], recv_sem=w_rs.at[p, st],
            device_id=device, device_id_type=MESH)

    def to_face(f):
        return (f, sub)

    def to_b(j):
        return (face, a_id * B + j)

    def to_a(j):
        return (face, j * B + b_id)

    def face_copy(p, f, f_in):
        part = sizes(p)[0]
        return remote(p, 0, spot(wb, p, f * part, part), w1in.at[f_in, whole(p, 0)], to_face(f))

    def b_copy(p, j, j_in):
        group = sizes(p)[1]
        at = pl.ds(pl.multiple_of(starts[p] // F + j * group, 16), group)
        return remote(p, 1, red.at[at, :], w2in.at[j_in, whole(p, 1)], to_b(j))

    def a_copy(p, j, j_in):
        return remote(p, 2, red2.at[whole(p, 1)], w3in.at[j_in, whole(p, 1)], to_a(j))

    def b_gather(p, j, own):
        part, group = sizes(p)
        place = spot(gath, p, face * part + own * group, group)
        return remote(p, 3, place, place, to_b(j))

    def face_gather(p, f, own):
        part = sizes(p)[0]
        place = spot(gath, p, own * part, part)
        return remote(p, 4, place, place, to_face(f))

    counts = (F - 1, B - 1, A - 1, B - 1, F - 1)

    def moved(p, st):
        return counts[st] * sizes(p)[(0, 1, 1, 1, 0)[st]]

    def arrived_all(p, st):
        if counts[st]:
            if st < 3:
                take((w1in, w2in, w3in)[st].at[0:counts[st], whole(p, st)], w_rs.at[p, st])
            else:
                take(gath.at[starts[p]:starts[p] + moved(p, st), :], w_rs.at[p, st])

    def reduce_start(p):
        peers(F, face, lambda f: face_copy(p, f, face).start())

    def summed(first, count, mine, ref, span):
        def step(d, tot):
            return tot + ref[lax.rem(mine + d, count), span, :].astype(F32)
        return lax.fori_loop(1, count, step, first)

    def reduce_b(p):
        arrived_all(p, 0)
        part, group = sizes(p)
        lo = starts[p] // F
        for r in range(B):
            tot = wf[pl.ds(pl.multiple_of(starts[p] + face * part + r * group, 16), group), :]
            for f in range(1, F):
                tot = tot + w1in[lax.rem(face + f, F), lo + r * group:lo + (r + 1) * group, :].astype(F32)
            accf[lo + r * group:lo + (r + 1) * group, :] = tot
            red[lo + r * group:lo + (r + 1) * group, :] = tot.astype(BF16)
        peers(B, b_id, lambda j: b_copy(p, j, b_id).start())

    def reduce_a(p):
        arrived_all(p, 1)
        group = sizes(p)[1]
        own = pl.ds(pl.multiple_of(starts[p] // F + b_id * group, 16), group)
        tot = summed(accf[own, :], B, b_id, w2in, whole(p, 1))
        red2[whole(p, 1), :] = tot.astype(BF16)
        peers(A, a_id, lambda j: a_copy(p, j, a_id).start())

    def gather_b(p):
        arrived_all(p, 2)
        part, group = sizes(p)
        tot = summed(red2[whole(p, 1), :].astype(F32), A, a_id, w3in, whole(p, 1))
        own = pl.ds(pl.multiple_of(starts[p] + face * part + b_id * group, 16), group)
        gath[own, :] = (tot * scale).astype(BF16)
        peers(B, b_id, lambda j: b_gather(p, j, b_id).start())

    def gather_face(p):
        arrived_all(p, 3)
        peers(F, face, lambda f: face_gather(p, f, face).start())

    def gather_end(p):
        arrived_all(p, 4)

    def drain():
        sent = sum(moved(p, st) for p in range(len(pieces)) for st in range(5))
        take(wf.at[0:sent // 2, :], w_ss.at[0])

    lines = 14 * C
    second_at = max(lines, starts[1])
    used = second_at + lines
    if wf.shape[0] > used:
        put(used, jnp.zeros((wf.shape[0] - used, LANES), F32))
    if second_at > lines:
        put(lines, jnp.zeros((second_at - lines, LANES), F32))
    early = [p for p in range(len(pieces)) if starts[p] + pieces[p] <= second_at]
    late = [p for p in range(len(pieces)) if p not in early]
    bias = jnp.sum(jnp.sum(gh, axis=0), axis=0, keepdims=True)
    line = iota((C, R), 0)
    blank = jnp.zeros((C, R), F32)
    spare = blank
    for q in range(C // R):
        spare = jnp.where(line == q, bias[:, q * R:(q + 1) * R], spare)
    weight_grad(0, win_in, gs1, spare)
    for p in early:
        reduce_start(p)

    half = (T + 2) // 2 * W
    conv(gs1, w1, pg, 0, half, True)
    reduce_b(0)
    halo1 = ex_wait(1, recv_mat, recv_low)
    add_halo(pad_act, halo1)
    windows(pad_act, win_act, T + 2)
    weight_grad(second_at, win_act, gs2, blank)
    for p in late:
        reduce_start(p)
    conv(win_act, w2, second, 0, M // 2, False)
    reduce_b(1)
    conv(win_act, w2, second, M // 2, M // 2, False)
    reduce_a(0)
    conv(gs1, w1, pg, half, MP - half, True)
    rims = dot(pad_rims, pg[...].astype(BF16)).astype(BF16)
    gact[...] = pg[...].reshape(T + 2, W, C)[1:T + 1]
    ex_start(3, recv_mat, recv_low, rims)
    hi, lo = split(second[...] + pad_in[1:T + 1, 1:W + 1, :].reshape(M, C))
    mean = hot(pool_pos(iota((1, M), 1)) == iota((H * 16, M), 0))
    down = (dot(mean, hi) + dot(mean, lo)) * 0.25
    pooled[...] = down.reshape(H, 16, C)[:, 0:H, :].astype(BF16)
    reduce_a(1)
    gather_b(0)
    gather_b(1)
    halo3 = ex_wait(3, send_mat, send_low)
    total = fold(gact, halo3) + gpad2[2:T + 2, 2:T + 2, :]
    gin[...] = total.astype(BF16)
    gather_face(0)
    gather_face(1)
    gather_end(0)
    gather_end(1)
    ex_drain()
    drain()


def finish(C, second_at, pooled_in, gin_in, gath, pooled, gin, gw1, gb1, gw2, wide, bias_row, sem):
    def out(i, src, dst):
        return pltpu.make_async_copy(src, dst, sem.at[i])

    copies = [out(0, pooled_in, pooled), out(1, gin_in, gin)]
    for c in copies:
        c.start()
    half = C - LANES
    for k, (base, dst) in enumerate(((0, gw1), (second_at, gw2))):
        for t in range(9):
            lo = base + t // 2 * 3 * C
            left = gath[lo + t % 2 * C:lo + t % 2 * C + C, :].astype(F32)
            lo = lo + (2 * C if t < 8 else C)
            pair = gath[lo:lo + C, :].astype(F32)
            right = pair[:, 0:half] if t % 2 == 0 else pair[:, half:2 * half]
            wide[k, t // 3, t % 3, :, 0:LANES] = left
            wide[k, t // 3, t % 3, :, LANES:C] = right
            copies.append(out(2 + k, wide.at[k, t // 3, t % 3], dst.at[t // 3, t % 3]))
            copies[-1].start()
    bias = gath[13 * C:13 * C + 16, :].astype(F32)
    for q in range(C // half):
        bias_row[:, q * half:(q + 1) * half] = bias[q:q + 1, half:2 * half]
    copies.append(out(4, bias_row, gb1))
    copies[-1].start()
    for k, dst in enumerate((gw1, gw2)):
        out(2 + k, wide.at[k], dst).wait()
    for c in copies[:2] + copies[-1:]:
        c.wait()


def local(S, F, features, w_first, b_first, w_second, neighbours, rotations, cotangent):
    T, C = features.shape[1], features.shape[2]
    H = T // 2
    D = neighbours.shape[0]
    A = 2 if S % 2 == 0 else 1
    B = S // A
    unit = 16 * F * B
    first = 14 * C // unit
    if first:
        units = (first, -(-28 * C // unit) - first)
    else:
        units = (1, -(-14 * C // unit))
    pieces = tuple(u * unit for u in units)
    rows = sum(pieces)
    K = S + 4 * F
    scale = 1.0 / math.sqrt(D * T * T)
    vm = pl.BlockSpec(memory_space=pltpu.VMEM)
    pooled, gin, gath = pl.pallas_call(
        functools.partial(kernel, S, F, pieces, scale),
        out_shape=(
            pltpu.VMEM((H, H, C), BF16),
            pltpu.VMEM((T, T, C), BF16),
            pltpu.VMEM((rows, LANES), BF16),
        ),
        in_specs=[pl.BlockSpec(memory_space=pl.ANY)] * 7,
        out_specs=(vm,) * 3,
        scratch_shapes=[
            pltpu.SMEM((4, D), jnp.int32),
            pltpu.SMEM((4, D), jnp.int32),
            pltpu.VMEM((T, T, C), BF16),
            pltpu.VMEM((H, H, C), BF16),
            pltpu.VMEM((9 * C, C), BF16),
            pltpu.VMEM((1, C), F32),
            pltpu.VMEM((9 * C, C), BF16),
            pltpu.VMEM((K * W, 4 * W), BF16),
            pltpu.VMEM((K * W, 4 * W), BF16),
            pltpu.VMEM((K * LOW, 8 * W), BF16),
            pltpu.VMEM((K * LOW, 8 * W), BF16),
            pltpu.VMEM((T + 2, W + 8, C), F32),
            pltpu.VMEM((T + 2, W + 8, C), F32),
            pltpu.VMEM((T + 4, W + 8, C), F32),
            pltpu.VMEM((T + 4, W + 8, C), F32),
            pltpu.VMEM((H, 16, C), F32),
            pltpu.VMEM((3, (T + 2) * W, C), BF16),
            pltpu.VMEM((3, (T + 2) * W, C), BF16),
            pltpu.VMEM((3, (T + 4) * W, C), BF16),
            pltpu.VMEM((3, (T + 4) * W, C), BF16),
            pltpu.VMEM((T * W, C), F32),
            pltpu.VMEM((T * W, C), F32),
            pltpu.VMEM(((T + 2) * W, C), F32),
            pltpu.VMEM((T, W, C), F32),
            pltpu.VMEM((4, K, T + LOW, LANES), BF16),
            pltpu.VMEM((4, K, T + LOW, LANES), BF16),
            pltpu.VMEM((rows, LANES), F32),
            pltpu.VMEM((rows, LANES), BF16),
            pltpu.VMEM((F, rows // F, LANES), BF16),
            pltpu.VMEM((rows // F, LANES), BF16),
            pltpu.VMEM((rows // F, LANES), F32),
            pltpu.VMEM((B, rows // (F * B), LANES), BF16),
            pltpu.VMEM((rows // (F * B), LANES), BF16),
            pltpu.VMEM((A, rows // (F * B), LANES), BF16),
            pltpu.SemaphoreType.DMA((1,)),
            pltpu.SemaphoreType.DMA((4,)),
            pltpu.SemaphoreType.DMA((1,)),
            pltpu.SemaphoreType.DMA((len(pieces), 5)),
            pltpu.SemaphoreType.DMA((7,)),
        ],
        compiler_params=pltpu.CompilerParams(
            collective_id=0, has_side_effects=True, vmem_limit_bytes=56 * 1024 * 1024
        ),
        name="level",
    )(
        neighbours.T, rotations.T, features, cotangent,
        w_first.reshape(9 * C, C), b_first.reshape(1, C), w_second.reshape(9 * C, C),
    )
    pooled, gin, gw1, gb1, gw2 = pl.pallas_call(
        functools.partial(finish, C, max(14 * C, pieces[0])),
        out_shape=(
            jax.ShapeDtypeStruct((H, H, C), BF16),
            jax.ShapeDtypeStruct((T, T, C), BF16),
            jax.ShapeDtypeStruct((3, 3, C, C), F32),
            jax.ShapeDtypeStruct((1, C), F32),
            jax.ShapeDtypeStruct((3, 3, C, C), F32),
        ),
        in_specs=[vm] * 3,
        out_specs=(pl.BlockSpec(memory_space=pl.ANY),) * 5,
        scratch_shapes=[
            pltpu.VMEM((2, 3, 3, C, C), F32),
            pltpu.VMEM((1, C), F32),
            pltpu.SemaphoreType.DMA((5,)),
        ],
        compiler_params=pltpu.CompilerParams(vmem_limit_bytes=24 * 1024 * 1024),
        name="finish",
    )(pooled, gin, gath)
    return (pooled, gin, gw1, gb1.reshape(C), gw2)


def solution(mesh):
    tiles = P(("face", "sub"), None, None)
    return jax.shard_map(
        functools.partial(local, mesh.shape["sub"], mesh.shape["face"]),
        mesh=mesh,
        in_specs=(tiles, P(), P(), P(), P(), P(), tiles),
        out_specs=(tiles, tiles, P(), P(), P()),
        check_vma=False,
    )
```
